256 devices in a mesh: dp: 64 (over z, y, core), seq: 4 (over x).
Axes of the slice: x: 4, y: 4, z: 8, core: 2. Of those that a mesh axis runs over, the one named last changes fastest.
Arguments:
- resid_in: bfloat16 [64, 2048, 512], P('dp', 'seq'), may hold values from -16 to 16
- conv_weight: bfloat16 [2, 1024, 1024], replicated, may hold values from -0.1875 to 0.1875
- out_weight: bfloat16 [2, 512, 1024], replicated, may hold values from -0.25 to 0.25
- resid_cot: bfloat16 [64, 2048, 512], P('dp', 'seq'), may hold values from -6 to 6
- skip_cot: bfloat16 [64, 2048, 512], P('dp', 'seq'), may hold values from -6 to 6
Outputs:
- conv_grad: float32 [2, 1024, 1024], P(None, 'dp')
- out_grad: float32 [2, 512, 1024], P(None, 'dp')
- resid_grad: bfloat16 [64, 2048, 512], P('dp', 'seq')
- skip_sum: bfloat16 [64, 2048, 512], P('dp', 'seq')
The draws below stay inside these ranges and needn't reach their ends.
All inputs are finite; a program needn't handle non-finite values.
Results may differ from the reference program's by a relative error of at most 0.014.
Values may be sent and summed in bfloat16 or wider, within the bound.
No kernel may reach another device: no remote copies, remote signals or barrier semaphores. Data moves between devices by JAX's collectives and lax.ppermute only.
A program may use at most 128 MiB of HBM per device.

```python
import jax
import jax.numpy as jnp
from jax import lax

C = 512
LAYERS = 2
DILATION = 128
LEN = 2048
BATCH = 64


def with_spikes(result, key, source, target, shards_of, factor):
    owner, partner = [(jnp.arange(result.shape[axis_at]) // (result.shape[axis_at] // shards_of)).reshape([-1 if axis == axis_at else 1 for axis in range(result.ndim)]) for axis_at in (source, target)]
    chosen = jax.random.permutation(key, shards_of)[partner]
    strong = (owner == chosen) | (owner == (partner + shards_of // 2) % shards_of)
    return jnp.where(strong, factor * result, result)


def block_levels(rng, dims, cuts, low, high):
    level = 1.0
    for axis_at, parts in cuts:
        heights = jax.random.uniform(jax.random.fold_in(jax.random.fold_in(rng, 6), axis_at), (parts,), jnp.float32, low / len(cuts), high / len(cuts))
        level = level * jnp.repeat(jnp.exp(heights), dims[axis_at] // parts).reshape((-1,) + (1,) * (len(dims) - 1 - axis_at))
    return level


def noise(key, extent, spread, reach, cuts=(), kind=jnp.bfloat16):
    loudness = block_levels(key, extent, cuts, -0.22, 0.18) if cuts else 1.0
    result = jax.random.normal(key, extent, jnp.float32) * spread * loudness
    return jnp.minimum(jnp.maximum(result, -reach), reach).astype(kind)


def noise_with(rng, dims, spread, limit, pieces, heavy, held_as=jnp.bfloat16):
    result = spread * jax.random.normal(rng, dims, jnp.float32)
    if pieces:
        result = result * block_levels(rng, dims, pieces, -0.22, 0.18)
    return jnp.clip(with_spikes(result, jax.random.fold_in(rng, 3), *heavy), -limit, limit).astype(held_as)


def setup_inputs(seed: int = 0) -> dict:
    keys = jax.random.split(jax.random.key(seed), 6)
    resid_in = noise_with(keys[0], (BATCH, LEN, C), 1.0, 16.0, ((0, 64), (1, 4)), (0, 2, 64, 4.0))
    conv_weight = noise(keys[1], (LAYERS, 2 * C, 2 * C), (2 * C) ** -0.5, 0.1875)
    out_weight = noise(keys[2], (LAYERS, C, 2 * C), C ** -0.5, 0.25)
    resid_cot = noise(keys[3], (BATCH, LEN, C), 1.0, 6.0, ((0, 64), (1, 4)))
    skip_cot = noise(keys[4], (BATCH, LEN, C), 1.0, 6.0, ((0, 64), (1, 4)))
    return dict(resid_in=resid_in, conv_weight=conv_weight, out_weight=out_weight, resid_cot=resid_cot, skip_cot=skip_cot)


def delay_rows(values, offset):
    return jnp.concatenate([jnp.zeros_like(values[:, :offset]), values[:, :values.shape[1] - offset]], axis=1)


def advance_rows(values, offset):
    return jnp.concatenate([values[:, offset:], jnp.zeros_like(values[:, :offset])], axis=1)


def reference(resid_in, conv_weight, out_weight, resid_cot, skip_cot):
    flat_rows = BATCH * LEN
    stream = resid_in
    kept_state = []
    skip_total = jnp.zeros((BATCH, LEN, C), jnp.float32)
    for ordinal in range(LAYERS):
        dilation_now = DILATION * 2 ** ordinal
        stacked = jnp.concatenate([delay_rows(stream, dilation_now), stream], axis=2).reshape(flat_rows, 2 * C)
        preact = jnp.dot(stacked, conv_weight[ordinal], preferred_element_type=jnp.float32)
        filter_act = jnp.tanh(preact[:, :C])
        gate_act = jax.nn.sigmoid(preact[:, C:])
        gated = (filter_act * gate_act).astype(jnp.bfloat16)
        projected = jnp.dot(gated, out_weight[ordinal], preferred_element_type=jnp.float32).reshape(BATCH, LEN, 2 * C)
        stream = (stream.astype(jnp.float32) + projected[:, :, :C]).astype(jnp.bfloat16)
        skip_total = skip_total + projected[:, :, C:]
        kept_state.append((stacked, filter_act, gate_act, gated))
    skip_sum = skip_total.astype(jnp.bfloat16)
    grad_flow = resid_cot.astype(jnp.float32)
    skip_rows = skip_cot.reshape(flat_rows, C)
    conv_terms = []
    out_terms = []
    contract_rows = (((0,), (0,)), ((), ()))
    contract_cols = (((1,), (1,)), ((), ()))
    for ordinal in reversed(range(LAYERS)):
        dilation_now = DILATION * 2 ** ordinal
        stacked, filter_act, gate_act, gated = kept_state[ordinal]
        proj_cot = jnp.concatenate([grad_flow.astype(jnp.bfloat16).reshape(flat_rows, C), skip_rows], axis=1)
        out_terms.append(lax.dot_general(gated, proj_cot, contract_rows, preferred_element_type=jnp.float32))
        gated_cot = lax.dot_general(proj_cot, out_weight[ordinal], contract_cols, preferred_element_type=jnp.float32)
        pre_cot = jnp.concatenate([gated_cot * (1.0 - filter_act * filter_act) * gate_act,
                                   gated_cot * filter_act * gate_act * (1.0 - gate_act)], axis=1).astype(jnp.bfloat16)
        conv_terms.append(lax.dot_general(stacked, pre_cot, contract_rows, preferred_element_type=jnp.float32))
        stack_cot = lax.dot_general(pre_cot, conv_weight[ordinal], contract_cols, preferred_element_type=jnp.float32).reshape(BATCH, LEN, 2 * C)
        grad_flow = grad_flow + stack_cot[:, :, C:] + advance_rows(stack_cot[:, :, :C], dilation_now)
    conv_grad = jnp.stack(conv_terms[::-1], axis=0)
    out_grad = jnp.stack(out_terms[::-1], axis=0)
    return conv_grad, out_grad, grad_flow.astype(jnp.bfloat16), skip_sum
```

```python
import jax
import jax.numpy as jnp
from jax import lax
from jax.sharding import Mesh, PartitionSpec as P

DILATION = 128
F32, BF16 = jnp.float32, jnp.bfloat16
Z, Y, CORES, X = 8, 4, 2, 4


def shifted(value, axis, steps, count):
    return lax.ppermute(value, axis, [(s, (s + steps) % count) for s in range(count)])


def exchange(parts, axis, count):
    me = lax.axis_index(axis)
    arrived = []
    for s in range(1, count):
        part = lax.dynamic_index_in_dim(parts, lax.rem(me + s, count), 0, False)
        arrived.append(shifted(part, axis, s, count))
    total = lax.dynamic_index_in_dim(parts, me, 0, False).astype(F32)
    for a in arrived:
        total = total + a.astype(F32)
    return total.astype(BF16)


def halve(parts, axis, partner, keep_high):
    size = len(partner)
    mine = jnp.where(keep_high, parts[1], parts[0])
    other = jnp.where(keep_high, parts[0], parts[1])
    got = lax.ppermute(other, axis, [(s, partner[s]) for s in range(size)])
    return mine.astype(F32) + got.astype(F32)


def spread(conv, out):
    g = jnp.concatenate(
        [conv.reshape(Z, Y, CORES, 16, 1024), out.reshape(Z, Y, CORES, 8, 1024)], axis=3
    ).astype(BF16)
    g = g.reshape(Z, Y, CORES, 24, 2, 4, 128).transpose(2, 4, 1, 5, 0, 3, 6)
    core = lax.axis_index("c")
    mine = lax.dynamic_index_in_dim(g, core, 0, False)
    other = lax.dynamic_index_in_dim(g, 1 - core, 0, False)
    got = lax.ppermute(other, "c", [(0, 1), (1, 0)])
    s = (mine.astype(F32) + got.astype(F32)).astype(BF16)
    a = exchange(s[0].transpose(1, 0, 2, 3, 4), "x", X)
    b = exchange(s[1], "y", Y)
    a = exchange(a, "y", Y)
    b = exchange(b, "x", X)
    return jnp.concatenate([a, b], axis=-1)


def finish(p):
    z = lax.axis_index("z")
    rows = p.shape[1]
    p = halve(p.reshape(2, 4, rows, 256), "z", [z_ ^ 4 for z_ in range(Z)], z >= 4)
    p = halve(p.astype(BF16).reshape(2, 2, rows, 256), "z", [z_ ^ 2 for z_ in range(Z)], (z & 2) > 0)
    p = halve(p.astype(BF16), "z", [z_ ^ 1 for z_ in range(Z)], (z & 1) > 0)
    p = p.astype(BF16)
    x = lax.axis_index("x")
    pieces = [p] + [shifted(p, "x", s, X) for s in range(1, X)]
    whole = jnp.stack(pieces)
    order = lax.rem(x - jnp.arange(X) + X, X)
    whole = whole[order]
    whole = whole.reshape(X, rows, 2, 128).transpose(1, 2, 0, 3).reshape(rows, 1024)
    return whole.astype(F32)


def along(value, steps):
    initial, last = (max(0, -steps), min(X, X - steps))
    return lax.ppermute(value, "x", [(s, s + steps) for s in range(initial, last)])


def on_device(resid_in, conv_weight, out_weight, resid_cot, skip_cot):
    x0 = resid_in[0]
    rc, sc = resid_cot[0], skip_cot[0]
    rows, ch = x0.shape
    d0, d1 = DILATION, 2 * DILATION
    halo = along(x0[rows - d0 - d1 :], 1)
    ext = jnp.concatenate([halo, x0])
    n0 = rows + d1
    stacked0 = jnp.concatenate([ext[:n0], ext[d0:]], axis=1)
    pre = jnp.dot(stacked0, conv_weight[0], preferred_element_type=F32)
    f0, g0 = jnp.tanh(pre[:, :ch]), jax.nn.sigmoid(pre[:, ch:])
    gated0 = (f0 * g0).astype(BF16)
    stream1 = (
        ext[d0:].astype(F32) + jnp.dot(gated0, out_weight[0][:, :ch], preferred_element_type=F32)
    ).astype(BF16)
    stacked0, f0, g0, gated0 = stacked0[d1:], f0[d1:], g0[d1:], gated0[d1:]
    stacked1 = jnp.concatenate([stream1[:rows], stream1[d1:]], axis=1)
    pre = jnp.dot(stacked1, conv_weight[1], preferred_element_type=F32)
    f1, g1 = jnp.tanh(pre[:, :ch]), jax.nn.sigmoid(pre[:, ch:])
    gated1 = (f1 * g1).astype(BF16)
    skip = jnp.dot(gated0, out_weight[0][:, ch:], preferred_element_type=F32) + jnp.dot(
        gated1, out_weight[1][:, ch:], preferred_element_type=F32
    )
    flow = rc.astype(F32)
    spreads = []
    kept = ((stacked0, f0, g0, gated0), (stacked1, f1, g1, gated1))
    rows_in = (((0,), (0,)), ((), ()))
    cols_in = (((1,), (1,)), ((), ()))
    for k in (1, 0):
        d = DILATION * 2**k
        stacked, f, g, gated = kept[k]
        pc = jnp.concatenate([flow.astype(BF16), sc], axis=1)
        gc = lax.dot_general(pc, out_weight[k], cols_in, preferred_element_type=F32)
        pre_cot = jnp.concatenate(
            [gc * (1.0 - f * f) * g, gc * f * g * (1.0 - g)], axis=1
        ).astype(BF16)
        st = lax.dot_general(pre_cot, conv_weight[k], cols_in, preferred_element_type=F32)
        back = along(st[:d, :ch].astype(BF16), -1).astype(F32)
        out_g = lax.dot_general(gated, pc, rows_in, preferred_element_type=F32)
        conv_g = lax.dot_general(stacked, pre_cot, rows_in, preferred_element_type=F32)
        flow = flow + st[:, ch:] + jnp.concatenate([st[d:, :ch], back])
        spreads.append(spread(conv_g, out_g))
    whole = finish(jnp.concatenate(spreads, axis=1))
    conv_grad = jnp.stack([whole[24:40], whole[:16]])
    out_grad = jnp.stack([whole[40:], whole[16:24]])
    return conv_grad, out_grad, flow.astype(BF16)[None], skip.astype(BF16)[None]


def solution(mesh):
    fine = Mesh(mesh.devices.reshape(Z, Y, CORES, X), ("z", "y", "c", "x"))
    dp = ("z", "y", "c")
    return jax.shard_map(
        on_device,
        mesh=fine,
        in_specs=(P(dp, "x", None), P(), P(), P(dp, "x", None), P(dp, "x", None)),
        out_specs=(
            P(None, dp, None),
            P(None, dp, None),
            P(dp, "x", None),
            P(dp, "x", None),
        ),
        check_vma=False,
    )
```

```python
import functools

import jax
import jax.numpy as jnp
from jax import lax
from jax.experimental import pallas as pl
from jax.experimental.pallas import tpu as pltpu
from jax.sharding import Mesh, PartitionSpec as P

F32, BF16 = jnp.float32, jnp.bfloat16
Z, Y, CORES, X = 8, 4, 2, 4
D0, D1 = 128, 256
ROWS, CH = 512, 512
HALO = D0 + D1
TILE = 256
VMEM_LIMIT = 56 * 1024 * 1024

FIRST, SECOND = (1, 0, 3, 2), (3, 2, 1, 0)
BIT_A, BIT_B = (0, 1, 1, 0), (0, 0, 1, 1)
Z_PAIRS = ((1, 0, 3, 2, 5, 4, 7, 6), (7, 2, 1, 4, 3, 6, 5, 0), (3, 6, 5, 0, 7, 2, 1, 4))
Z_ORDER = (0, 3, 7, 4, 1, 6, 2, 5)


def ring_place(i, half):
    a, b = BIT_A[i], BIT_B[i]
    return 2 * a + b if half == 0 else 2 * b + a


def dot(a, b):
    return jnp.dot(a, b, preferred_element_type=F32)


def dot_cols(a, b):
    return lax.dot_general(a, b, (((1,), (1,)), ((), ())), preferred_element_type=F32)


def dot_rows(a, b):
    return lax.dot_general(a, b, (((0,), (0,)), ((), ())), preferred_element_type=F32)


def gates(pre):
    return jnp.tanh(pre[:, :CH]), 0.5 * jnp.tanh(0.5 * pre[:, CH:]) + 0.5


def forward_kernel(
    ext, cw, ow, rc, sc,
    early, flow, pre1, stream1, gated0, gated1, slope_f, slope_g, skip,
    skip_acc,
):
    for r in range(0, ROWS + D1, TILE):
        now = ext[D0 + r : D0 + r + TILE, :]
        pre = dot(ext[r : r + TILE, :], cw[0, :CH, :]) + dot(now, cw[0, CH:, :])
        f, g = gates(pre)
        gated = (f * g).astype(BF16)
        stream1[r : r + TILE, :] = (now.astype(F32) + dot(gated, ow[0, :, :CH])).astype(BF16)
        if r >= D1:
            at = slice(r - D1, r - D1 + TILE)
            gated0[at, :] = gated
            slope_f[at, :] = (1.0 - f * f) * g
            slope_g[at, :] = f * g * (1.0 - g)
            skip_acc[at, :] = dot(gated, ow[0, :, CH:])
    for r in range(0, ROWS, TILE):
        at = slice(r, r + TILE)
        pre = dot(stream1[at, :], cw[1, :CH, :]) + dot(stream1[r + D1 : r + D1 + TILE, :], cw[1, CH:, :])
        f, g = gates(pre)
        gated = (f * g).astype(BF16)
        gated1[at, :] = gated
        skip[at, :] = (skip_acc[at, :] + dot(gated, ow[1, :, CH:])).astype(BF16)
        gc = dot_cols(rc[at, :], ow[1, :, :CH]) + dot_cols(sc[at, :], ow[1, :, CH:])
        pre1[at, :CH] = (gc * ((1.0 - f * f) * g)).astype(BF16)
        pre1[at, CH:] = (gc * (f * g * (1.0 - g))).astype(BF16)
        pc = pre1[at, :]
        flow[at, :] = rc[at, :].astype(F32) + dot_cols(pc, cw[1, CH:, :])
        ahead = dot_cols(pc, cw[1, :CH, :])
        if r < D1:
            early[at, :] = ahead.astype(BF16)
        else:
            flow[r - D1 : r - D1 + TILE, :] += ahead


def backward_kernel(flow1, returned, slope_f, slope_g, sc, ow, cw, proj, pre0, flow, early):
    for r in range(0, ROWS, TILE):
        at = slice(r, r + TILE)
        fl = flow1[at, :]
        if r + TILE > ROWS - D1:
            fl = fl + returned[r - (ROWS - D1) : r - (ROWS - D1) + TILE, :].astype(F32)
        flow_b = fl.astype(BF16)
        proj[at, :] = flow_b
        gc = dot_cols(flow_b, ow[0, :, :CH]) + dot_cols(sc[at, :], ow[0, :, CH:])
        pre0[at, :CH] = (gc * slope_f[at, :]).astype(BF16)
        pre0[at, CH:] = (gc * slope_g[at, :]).astype(BF16)
        pc = pre0[at, :]
        flow[at, :] = fl + dot_cols(pc, cw[0, CH:, :])
        ahead = dot_cols(pc, cw[0, :CH, :])
        if r == 0:
            early[...] = ahead[:D0, :].astype(BF16)
            flow[: TILE - D0, :] += ahead[D0:, :]
        else:
            flow[r - D0 : r - D0 + TILE, :] += ahead


def gradient_kernel(layer, core, stream, gated, pre, left, right, mine, other):
    delay = D0 if layer == 0 else D1
    odd = jnp.full((16, 128), core[0], jnp.int32) == 1
    odd_8 = jnp.full((8, 128), core[0], jnp.int32) == 1

    def place(half, y, block):
        return (half, block, ring_place(y, 0)) if layer == 1 else (half, ring_place(y, half), block)

    for n in range(4):
        half = n // 2
        cot = pre[:, n * 256 : (n + 1) * 256]
        for m in range(4):
            start = 0 if m < 2 else delay
            lhs = stream[start : start + ROWS, (m % 2) * 256 : (m % 2) * 256 + 256]
            g = dot_rows(lhs, cot)
            for dz in range(2):
                unit, t = divmod(Z_ORDER.index(m * 2 + dz), 2)
                for y in range(Y):
                    row = dz * 128 + y * 32
                    for b in range(2):
                        at = place(half, y, 2 * (n % 2) + b) + (unit, slice(t * 16, t * 16 + 16))
                        even = g[row : row + 16, b * 128 : b * 128 + 128]
                        uneven = g[row + 16 : row + 32, b * 128 : b * 128 + 128]
                        mine[at] = jnp.where(odd, uneven, even).astype(BF16)
                        other[at] = jnp.where(odd, even, uneven).astype(BF16)
        side = left if n < 2 else right
        g = dot_rows(gated[...], side[:, (n % 2) * 256 : (n % 2) * 256 + 256])
        for unit in range(4):
            for y in range(Y):
                for b in range(2):
                    at = place(half, y, 2 * (n % 2) + b) + (unit, slice(32, 48))
                    mine_parts, other_parts = [], []
                    for t in range(2):
                        row = Z_ORDER[unit * 2 + t] * 64 + y * 16
                        even = g[row : row + 8, b * 128 : b * 128 + 128]
                        uneven = g[row + 8 : row + 16, b * 128 : b * 128 + 128]
                        mine_parts.append(jnp.where(odd_8, uneven, even))
                        other_parts.append(jnp.where(odd_8, even, uneven))
                    mine[at] = jnp.concatenate(mine_parts, axis=0).astype(BF16)
                    other[at] = jnp.concatenate(other_parts, axis=0).astype(BF16)


def kernel_call(kernel, shapes, args, flops, moved, scratch=(), smem=0):
    vmem = pl.BlockSpec(memory_space=pltpu.VMEM)
    return pl.pallas_call(
        kernel,
        out_shape=[jax.ShapeDtypeStruct(s, t) for s, t in shapes],
        in_specs=[pl.BlockSpec(memory_space=pltpu.SMEM)] * smem + [vmem] * (len(args) - smem),
        out_specs=[vmem] * len(shapes),
        scratch_shapes=scratch,
        compiler_params=pltpu.CompilerParams(vmem_limit_bytes=VMEM_LIMIT),
        cost_estimate=pl.CostEstimate(flops=flops, bytes_accessed=moved, transcendentals=0),
    )(*args)


def table(values, i):
    return jnp.asarray(values, jnp.int32)[i]


def halve(parts, axis, pairs, bit):
    kept = lax.dynamic_index_in_dim(parts, bit, 0, False)
    sent = lax.dynamic_index_in_dim(parts, 1 - bit, 0, False)
    got = lax.ppermute(sent, axis, list(enumerate(pairs)))
    return (kept.astype(F32) + got.astype(F32)).astype(BF16)


def core_sum(mine, other):
    got = lax.ppermute(other, "c", [(0, 1), (1, 0)])
    return (mine.astype(F32) + got.astype(F32)).astype(BF16)


def ring_first(s, axis, bit_a, bit_b):
    rest = s.shape[2:]
    one = halve(s[0].reshape((2, 2) + rest), axis, FIRST, bit_a)
    two = halve(s[1].reshape((2, 2) + rest), axis, SECOND, bit_b)
    one = halve(one, axis, SECOND, bit_b)
    two = halve(two, axis, FIRST, bit_a)
    return one, two


def ring_last(one, two, axis, bit_a, bit_b):
    s = jnp.stack([one, two], axis=1)
    s = s.reshape((2, 2) + s.shape[1:])
    s = halve(s, axis, FIRST, bit_a)
    return halve(s, axis, SECOND, bit_b)


def along(value, steps):
    initial, last = (max(0, -steps), min(X, X - steps))
    return lax.ppermute(value, "x", [(s, s + steps) for s in range(initial, last)])


def on_device(resid_in, conv_weight, out_weight, resid_cot, skip_cot):
    x0, rc, sc = resid_in[0], resid_cot[0], skip_cot[0]
    core = lax.axis_index("c").astype(jnp.int32)[None]
    xi, yi, zi = (lax.axis_index(a) for a in ("x", "y", "z"))
    xa, xb, ya, yb = table(BIT_A, xi), table(BIT_B, xi), table(BIT_A, yi), table(BIT_B, yi)
    ext = jnp.concatenate([along(x0[ROWS - HALO :], 1), x0])
    early1, flow1, pre1, stream1, gated0, gated1, slope_f, slope_g, skip = kernel_call(
        forward_kernel,
        [((D1, CH), BF16), ((ROWS, CH), F32), ((ROWS, 2 * CH), BF16), ((ROWS + D1, CH), BF16)]
        + [((ROWS, CH), BF16)] * 2
        + [((ROWS, CH), F32)] * 2
        + [((ROWS, CH), BF16)],
        (ext, conv_weight, out_weight, rc, sc),
        6 * 10**9,
        10**7,
        [pltpu.VMEM((ROWS, CH), F32)],
    )
    returned1 = along(early1, -1)
    pieces = (2, 4, 4, 4, 48, 128)
    shapes = [(pieces, BF16)] * 2
    mine1, other1 = kernel_call(
        functools.partial(gradient_kernel, 1), shapes, (core, stream1, gated1, pre1, rc, sc), 16 * 10**8, 6 * 10**6, smem=1
    )
    proj0, pre0, flow0, early0 = kernel_call(
        backward_kernel,
        [((ROWS, CH), BF16), ((ROWS, 2 * CH), BF16), ((ROWS, CH), F32), ((D0, CH), BF16)],
        (flow1, returned1, slope_f, slope_g, sc, out_weight, conv_weight),
        16 * 10**8,
        6 * 10**6,
    )
    returned0 = along(early0, -1)
    mine0, other0 = kernel_call(
        functools.partial(gradient_kernel, 0),
        shapes,
        (core, ext[D1:], gated0, pre0, proj0, sc),
        16 * 10**8,
        6 * 10**6,
        smem=1,
    )
    resid = jnp.concatenate([flow0[: ROWS - D0], flow0[ROWS - D0 :] + returned0.astype(F32)]).astype(BF16)

    s1 = core_sum(mine1, other1)
    s0 = core_sum(mine0, other0)
    one1, two1 = ring_first(s1, "x", xa, xb)
    one0, two0 = ring_first(s0, "y", ya, yb)
    s1 = ring_last(one1, two1, "y", ya, yb)
    s0 = ring_last(one0, two0, "x", xa, xb)
    s = jnp.stack([s1, s0]).transpose(2, 0, 1, 3, 4)
    place = table([Z_ORDER.index(i) for i in range(Z)], zi)
    s = halve(s.reshape((2, 2) + s.shape[1:]), "z", Z_PAIRS[0], place // 4)
    s = halve(s, "z", Z_PAIRS[1], (place // 2) % 2)
    conv, out = s[:, :, :32].reshape(2, 2, 2, 16, 128), s[:, :, 32:].reshape(2, 2, 2, 8, 128)
    s = halve(jnp.concatenate([conv, out], axis=3).transpose(2, 0, 1, 3, 4), "z", Z_PAIRS[2], place % 2)
    parts = [s] + [lax.ppermute(s, "x", [(i, (i + k) % X) for i in range(X)]) for k in range(1, X)]
    whole = jnp.stack(parts)
    layer_rows = []
    for slot, layer in ((0, 1), (1, 0)):
        halves = []
        for half in range(2):
            source = [[ring_place(i, half if layer == 1 else 0) for i in range(X)].index(b) for b in range(X)]
            picks = lax.rem(xi - jnp.asarray(source) + X, X)
            halves.append(whole[picks, slot, half].transpose(1, 0, 2).reshape(24, 512))
        layer_rows.append(jnp.concatenate(halves, axis=1).astype(F32))
    conv_grad = jnp.stack([layer_rows[1][:16], layer_rows[0][:16]])
    out_grad = jnp.stack([layer_rows[1][16:], layer_rows[0][16:]])
    return conv_grad, out_grad, resid[None], skip[None]


def solution(mesh):
    fine = Mesh(mesh.devices.reshape(Z, Y, CORES, X), ("z", "y", "c", "x"))
    dp = ("z", "y", "c")
    return jax.shard_map(
        on_device,
        mesh=fine,
        in_specs=(P(dp, "x", None), P(), P(), P(dp, "x", None), P(dp, "x", None)),
        out_specs=(P(None, dp, None), P(None, dp, None), P(dp, "x", None), P(dp, "x", None)),
        check_vma=False,
    )
```

```python
import functools

import jax
import jax.numpy as jnp
from jax import lax
from jax.experimental import pallas as pl
from jax.experimental.pallas import tpu as pltpu
from jax.sharding import Mesh, PartitionSpec as P

F32, BF16 = jnp.float32, jnp.bfloat16
Z, Y, CORES, X = 8, 4, 2, 4
D0, D1 = 128, 256
ROWS, CH = 512, 512
HALO = D0 + D1
TILE = 256
MIB = 1024 * 1024

FIRST, SECOND = (1, 0, 3, 2), (3, 2, 1, 0)
BIT_A, BIT_B = (0, 1, 1, 0), (0, 0, 1, 1)
Z_PAIRS = ((1, 0, 3, 2, 5, 4, 7, 6), (7, 2, 1, 4, 3, 6, 5, 0), (3, 6, 5, 0, 7, 2, 1, 4))
Z_ORDER = (0, 3, 7, 4, 1, 6, 2, 5)
Z_ORDERS = (Z_ORDER, tuple((i + 1) % Z for i in Z_ORDER))
Z_PAIRS_NEXT = tuple(tuple((pairs[(i - 1) % Z] + 1) % Z for i in range(Z)) for pairs in Z_PAIRS)
Z_SECOND, Z_THIRD = (sum(((Z_ORDER.index(i) >> k) & 1) << i for i in range(Z)) for k in (1, 0))


def ring_place(i, half):
    a, b = BIT_A[i], BIT_B[i]
    return 2 * a + b if half == 0 else 2 * b + a


def dot(a, b):
    return jnp.dot(a, b, preferred_element_type=F32)


def dot_cols(a, b):
    return lax.dot_general(a, b, (((1,), (1,)), ((), ())), preferred_element_type=F32)


def dot_rows(a, b):
    return lax.dot_general(a, b, (((0,), (0,)), ((), ())), preferred_element_type=F32)


def gates(pre):
    return jnp.tanh(pre[:, :CH]), 0.5 * jnp.tanh(0.5 * pre[:, CH:]) + 0.5


def forward_local_kernel(local, cw, ow, stream, gated0, slope_f, slope_g, skip):
    for r, size in ((D0, D0), (2 * D0, TILE)):
        at = slice(r - D0, r - D0 + size)
        now = local[r : r + size, :]
        pre = dot(local[at, :], cw[0, :CH, :]) + dot(now, cw[0, CH:, :])
        f, g = gates(pre)
        gated = (f * g).astype(BF16)
        stream[at, :] = (now.astype(F32) + dot(gated, ow[0, :, :CH])).astype(BF16)
        gated0[at, :] = gated
        slope_f[at, :] = (1.0 - f * f) * g
        slope_g[at, :] = f * g * (1.0 - g)
        skip[at, :] = dot(gated, ow[0, :, CH:])


def forward_kernel(
    halo, local, cw, ow, rc, sc, stream_high, skip_high,
    early, flow, pre1, stream1, gated0, gated1, slope_f, slope_g, skip,
    ext, skip_low,
):
    ext[:HALO, :] = halo[...]
    ext[HALO:, :] = local[:D0, :]
    for r, size in ((0, TILE), (D1, D0)):
        now = ext[D0 + r : D0 + r + size, :]
        pre = dot(ext[r : r + size, :], cw[0, :CH, :]) + dot(now, cw[0, CH:, :])
        f, g = gates(pre)
        gated = (f * g).astype(BF16)
        stream1[r : r + size, :] = (now.astype(F32) + dot(gated, ow[0, :, :CH])).astype(BF16)
        if r == D1:
            gated0[...] = gated
            slope_f[...] = (1.0 - f * f) * g
            slope_g[...] = f * g * (1.0 - g)
            skip_low[...] = dot(gated, ow[0, :, CH:])
    stream1[HALO:, :] = stream_high[...]
    for r in range(0, ROWS, TILE):
        at = slice(r, r + TILE)
        pre = dot(stream1[at, :], cw[1, :CH, :]) + dot(stream1[r + D1 : r + D1 + TILE, :], cw[1, CH:, :])
        f, g = gates(pre)
        gated = (f * g).astype(BF16)
        gated1[at, :] = gated
        more = dot(gated, ow[1, :, CH:])
        if r == 0:
            skip[:D0, :] = (skip_low[...] + more[:D0, :]).astype(BF16)
            skip[D0:TILE, :] = (skip_high[:D0, :] + more[D0:, :]).astype(BF16)
        else:
            skip[at, :] = (skip_high[D0:, :] + more).astype(BF16)
        gc = dot_cols(rc[at, :], ow[1, :, :CH]) + dot_cols(sc[at, :], ow[1, :, CH:])
        pre1[at, :CH] = (gc * ((1.0 - f * f) * g)).astype(BF16)
        pre1[at, CH:] = (gc * (f * g * (1.0 - g))).astype(BF16)
        pc = pre1[at, :]
        flow[at, :] = rc[at, :].astype(F32) + dot_cols(pc, cw[1, CH:, :])
        ahead = dot_cols(pc, cw[1, :CH, :])
        if r < D1:
            early[at, :] = ahead.astype(BF16)
        else:
            flow[:TILE, :] += ahead


def backward_low_kernel(flow1, low_f, low_g, high_f, high_g, sc, ow, cw, proj, pre0, flow, early):
    fl = flow1[:TILE, :]
    flow_b = fl.astype(BF16)
    proj[...] = flow_b
    gc = dot_cols(flow_b, ow[0, :, :CH]) + dot_cols(sc[:TILE, :], ow[0, :, CH:])
    pre0[:D0, :CH] = (gc[:D0] * low_f[...]).astype(BF16)
    pre0[:D0, CH:] = (gc[:D0] * low_g[...]).astype(BF16)
    pre0[D0:, :CH] = (gc[D0:] * high_f[:D0, :]).astype(BF16)
    pre0[D0:, CH:] = (gc[D0:] * high_g[:D0, :]).astype(BF16)
    pc = pre0[...]
    flow[...] = fl + dot_cols(pc, cw[0, CH:, :])
    ahead = dot_cols(pc, cw[0, :CH, :])
    early[...] = ahead[:D0, :].astype(BF16)
    flow[:D0, :] += ahead[D0:, :]


def backward_high_kernel(flow1, returned, high_f, high_g, sc, ow, cw, flow_low, proj, pre0, resid, tail):
    fl = flow1[TILE:, :] + returned[...].astype(F32)
    flow_b = fl.astype(BF16)
    proj[...] = flow_b
    gc = dot_cols(flow_b, ow[0, :, :CH]) + dot_cols(sc[TILE:, :], ow[0, :, CH:])
    pre0[:, :CH] = (gc * high_f[D0:, :]).astype(BF16)
    pre0[:, CH:] = (gc * high_g[D0:, :]).astype(BF16)
    pc = pre0[...]
    fl = fl + dot_cols(pc, cw[0, CH:, :])
    ahead = dot_cols(pc, cw[0, :CH, :])
    resid[:D0, :] = flow_low[:D0, :].astype(BF16)
    resid[D0:TILE, :] = (flow_low[D0:, :] + ahead[:D0, :]).astype(BF16)
    resid[TILE:, :] = (fl[:D0, :] + ahead[D0:, :]).astype(BF16)
    tail[...] = fl[D0:, :]


def place(layer, half, y, z):
    order = Z_ORDERS[half] if layer == 1 else Z_ORDER
    unit, t = divmod(order.index(z), 2)
    if layer == 1:
        return (unit, ring_place(y, 0)), t
    return (ring_place(y, half), unit), t


def gradient_body(core, layer, stream, gated, pre, left, right, mine, other):
    delay = D1 if layer == 1 else D0
    odd = jnp.full((16, CH // 2), core[0], jnp.int32) == 1
    odd_8 = jnp.full((8, CH // 2), core[0], jnp.int32) == 1
    for n in range(4):
        half = n // 2
        cols = slice((n % 2) * 256, (n % 2) * 256 + 256)
        cot = pre[:, n * 256 : (n + 1) * 256]
        for m in range(4):
            start = 0 if m < 2 else delay
            lhs = stream[start : start + ROWS, (m % 2) * 256 : (m % 2) * 256 + 256]
            g = dot_rows(lhs, cot)
            for dz in range(2):
                for y in range(Y):
                    row = dz * 128 + y * 32
                    where, t = place(layer, half, y, m * 2 + dz)
                    at = (half, *where, slice(t * 16, t * 16 + 16), cols)
                    even, uneven = g[row : row + 16], g[row + 16 : row + 32]
                    mine[at] = jnp.where(odd, uneven, even).astype(BF16)
                    other[at] = jnp.where(odd, even, uneven).astype(BF16)
        side = left if n < 2 else right
        g = dot_rows(gated[...], side[:, cols])
        order = Z_ORDERS[half] if layer == 1 else Z_ORDER
        for unit in range(4):
            for y in range(Y):
                where, _ = place(layer, half, y, order[2 * unit])
                at = (half, *where, slice(32, 48), cols)
                mine_parts, other_parts = [], []
                for t in range(2):
                    row = order[unit * 2 + t] * 64 + y * 16
                    even, uneven = g[row : row + 8], g[row + 8 : row + 16]
                    mine_parts.append(jnp.where(odd_8, uneven, even))
                    other_parts.append(jnp.where(odd_8, even, uneven))
                mine[at] = jnp.concatenate(mine_parts, axis=0).astype(BF16)
                other[at] = jnp.concatenate(other_parts, axis=0).astype(BF16)


def gradient_1_kernel(core, stream, gated, pre, left, right, mine, other):
    gradient_body(core, 1, stream, gated, pre, left, right, mine, other)


def gradient_0_kernel(
    core, halo, local, gated_low, gated_high, pre_low, pre_high, left_low, left_high, right,
    mine, other,
    stream, gated, pre, left,
):
    stream[:D0, :] = halo[D1:, :]
    stream[D0:, :] = local[...]
    gated[:D0, :] = gated_low[...]
    gated[D0:, :] = gated_high[...]
    pre[:TILE, :] = pre_low[...]
    pre[TILE:, :] = pre_high[...]
    left[:TILE, :] = left_low[...]
    left[TILE:, :] = left_high[...]
    gradient_body(core, 0, stream, gated, pre, left, right, mine, other)


def kernel_call(kernel, shapes, args, flops, moved, limit, scratch=(), smem=0):
    vmem = pl.BlockSpec(memory_space=pltpu.VMEM)
    return pl.pallas_call(
        kernel,
        out_shape=[jax.ShapeDtypeStruct(s, t) for s, t in shapes],
        in_specs=[pl.BlockSpec(memory_space=pltpu.SMEM)] * smem + [vmem] * (len(args) - smem),
        out_specs=[vmem] * len(shapes),
        scratch_shapes=scratch,
        compiler_params=pltpu.CompilerParams(vmem_limit_bytes=limit * MIB),
        cost_estimate=pl.CostEstimate(flops=flops, bytes_accessed=moved, transcendentals=0),
    )(*args)


def halve(parts, axis, pairs, bit):
    kept = lax.dynamic_index_in_dim(parts, bit, 0, False, allow_negative_indices=False)
    sent = lax.dynamic_index_in_dim(parts, 1 - bit, 0, False, allow_negative_indices=False)
    got = lax.ppermute(sent, axis, list(enumerate(pairs)))
    return (kept.astype(F32) + got.astype(F32)).astype(BF16)


def core_sum(mine, other):
    got = lax.ppermute(other, "c", [(0, 1), (1, 0)])
    return (mine.astype(F32) + got.astype(F32)).astype(BF16)


def split(s):
    return s.reshape((2, 2) + s.shape[1:])


def split_last(s):
    lead = s.shape[:-2]
    conv, out = s[..., :32, :].reshape(*lead, 2, 16, CH), s[..., 32:, :].reshape(*lead, 2, 8, CH)
    return jnp.moveaxis(jnp.concatenate([conv, out], axis=-2), -3, 0)


def together(a, b):
    return lax.optimization_barrier((a, b))


def from_x(s):
    return [lax.ppermute(s, "x", [(i, (i + k) % X) for i in range(X)]) for k in (2, 1, 3)]


def along(value, steps):
    initial, last = (max(0, -steps), min(X, X - steps))
    return lax.ppermute(value, "x", [(s, s + steps) for s in range(initial, last)])


def assemble_kernel(own, opposite, one, two, conv, out):
    for layer in range(2):
        for half in range(2):
            i = 2 * layer + half
            at = slice(half * CH, half * CH + CH)
            piece = (own[i].astype(F32) + opposite[i].astype(F32)) + (one[i].astype(F32) + two[i].astype(F32))
            conv[layer, :, at] = piece[:16]
            out[layer, :, at] = piece[16:]


def ring_bits(i):
    b = i >> 1
    return (i + b) & 1, b


def on_device(resid_in, conv_weight, out_weight, resid_cot, skip_cot):
    x0, rc, sc = resid_in[0], resid_cot[0], skip_cot[0]
    core = lax.axis_index("c")[None]
    yi, zi = lax.axis_index("y"), lax.axis_index("z")
    ya, yb = ring_bits(yi)
    z_bits = [(((i + 1) >> 1) & 1, (Z_SECOND >> i) & 1, (Z_THIRD >> i) & 1) for i in (zi, (zi - 1) & (Z - 1))]
    high = ROWS - D0
    halo = along(x0[ROWS - HALO :], 1)
    stream_high, gated_high, high_f, high_g, skip_high = kernel_call(
        forward_local_kernel,
        [((high, CH), BF16)] * 2 + [((high, CH), F32)] * 3,
        (x0, conv_weight, out_weight),
        12 * 10**8,
        10**7,
        16,
    )
    halo, high_f = lax.optimization_barrier((halo, high_f))
    early1, flow1, pre1, stream1, gated_low, gated1, low_f, low_g, skip = kernel_call(
        forward_kernel,
        [((D1, CH), BF16), ((ROWS, CH), F32), ((ROWS, 2 * CH), BF16), ((ROWS + D1, CH), BF16)]
        + [((D0, CH), BF16), ((ROWS, CH), BF16)]
        + [((D0, CH), F32)] * 2
        + [((ROWS, CH), BF16)],
        (halo, x0, conv_weight, out_weight, rc, sc, stream_high, skip_high),
        4 * 10**9,
        10**7,
        20,
        [pltpu.VMEM((HALO + D0, CH), BF16), pltpu.VMEM((D0, CH), F32)],
    )
    returned1 = along(early1, -1)
    pieces = (4, 4, 48, CH)
    mine1, other1 = kernel_call(
        gradient_1_kernel,
        [((2,) + pieces, BF16)] * 2,
        (core, stream1, gated1, pre1, rc, sc),
        5 * 10**9,
        6 * 10**6,
        16,
        smem=1,
    )
    proj_low, pre_low, flow_low, early0 = kernel_call(
        backward_low_kernel,
        [((TILE, CH), BF16), ((TILE, 2 * CH), BF16), ((TILE, CH), F32), ((D0, CH), BF16)],
        (flow1, low_f, low_g, high_f, high_g, sc, out_weight, conv_weight),
        25 * 10**8,
        6 * 10**6,
        16,
    )
    returned1, mine1, other1, flow_low = lax.optimization_barrier((returned1, mine1, other1, flow_low))
    returned0 = along(early0, -1)
    proj_high, pre_high, resid_most, tail = kernel_call(
        backward_high_kernel,
        [((TILE, CH), BF16), ((TILE, 2 * CH), BF16), ((high, CH), BF16), ((D0, CH), F32)],
        (flow1, returned1, high_f, high_g, sc, out_weight, conv_weight, flow_low),
        25 * 10**8,
        6 * 10**6,
        16,
    )
    sums1 = core_sum(mine1, other1)
    mine0, other0 = kernel_call(
        gradient_0_kernel,
        [((2,) + pieces, BF16)] * 2,
        (core, halo, x0, gated_low, gated_high, pre_low, pre_high, proj_low, proj_high, sc),
        5 * 10**9,
        6 * 10**6,
        16,
        [pltpu.VMEM((ROWS + D0, CH), BF16), pltpu.VMEM((ROWS, CH), BF16)]
        + [pltpu.VMEM((ROWS, 2 * CH), BF16), pltpu.VMEM((ROWS, CH), BF16)],
        smem=1,
    )
    sums0 = core_sum(mine0, other0)
    resid = jnp.concatenate([resid_most, (tail + returned0.astype(F32)).astype(BF16)])

    pairs_1 = (Z_PAIRS, Z_PAIRS_NEXT)
    y_steps = ((FIRST, ya), (SECOND, yb))
    s1 = [halve(split(sums1[half]), "z", pairs_1[half][0], z_bits[half][0]) for half in range(2)]
    s0 = [halve(split(sums0[half]), "y", *y_steps[half]) for half in range(2)]
    s0, s1 = together(s0, s1)
    s0 = [halve(s0[half], "y", *y_steps[1 - half]) for half in range(2)]
    s1 = [halve(s1[half], "z", pairs_1[half][1], z_bits[half][1]) for half in range(2)]
    s0, s1 = together(s0, s1)
    s0 = halve(split(jnp.stack(s0, axis=1)), "z", Z_PAIRS[0], z_bits[0][0])
    s1 = halve(split(jnp.stack(s1, axis=1)), "y", *y_steps[0])
    s0, s1 = together(s0, s1)
    s0 = halve(s0, "z", Z_PAIRS[1], z_bits[0][1])
    s1 = halve(s1, "y", *y_steps[1])
    most, least = together(jnp.concatenate([s0, s1[:1]]), s1[1:])
    most = halve(split_last(most), "z", Z_PAIRS[2], z_bits[0][2])
    least = halve(split_last(least), "z", Z_PAIRS_NEXT[2], z_bits[1][2])
    s = jnp.concatenate([most, least])
    conv_grad, out_grad = kernel_call(
        assemble_kernel,
        [((2, 16, 1024), F32), ((2, 8, 1024), F32)],
        [s] + from_x(s),
        10**6,
        10**6,
        8,
    )
    return conv_grad, out_grad, resid[None], skip[None]


def solution(mesh):
    fine = Mesh(mesh.devices.reshape(Z, Y, CORES, X), ("z", "y", "c", "x"))
    dp = ("z", "y", "c")
    return jax.shard_map(
        on_device,
        mesh=fine,
        in_specs=(P(dp, "x", None), P(), P(), P(dp, "x", None), P(dp, "x", None)),
        out_specs=(P(None, dp, None), P(None, dp, None), P(dp, "x", None), P(dp, "x", None)),
        check_vma=False,
    )
```

```python
import functools

import jax
import jax.numpy as jnp
from jax import lax
from jax.experimental import pallas as pl
from jax.experimental.pallas import tpu as pltpu
from jax.sharding import Mesh, PartitionSpec as P

F32, BF16 = jnp.float32, jnp.bfloat16
Z, Y, CORES, X = 8, 4, 2, 4
D0, D1 = 128, 256
ROWS, CH = 512, 512
HALO = D0 + D1
TILE = 256
MIB = 1024 * 1024

FIRST, SECOND = (1, 0, 3, 2), (3, 2, 1, 0)
BIT_A, BIT_B = (0, 1, 1, 0), (0, 0, 1, 1)
Z_PAIRS = ((1, 0, 3, 2, 5, 4, 7, 6), (7, 2, 1, 4, 3, 6, 5, 0), (3, 6, 5, 0, 7, 2, 1, 4))
Z_ORDER = (0, 3, 7, 4, 1, 6, 2, 5)
Z_ORDERS = (Z_ORDER, tuple((i + 1) % Z for i in Z_ORDER))
Z_PAIRS_NEXT = tuple(tuple((pairs[(i - 1) % Z] + 1) % Z for i in range(Z)) for pairs in Z_PAIRS)
Z_SECOND, Z_THIRD = (sum(((Z_ORDER.index(i) >> k) & 1) << i for i in range(Z)) for k in (1, 0))


def ring_place(i, half):
    a, b = BIT_A[i], BIT_B[i]
    return 2 * a + b if half == 0 else 2 * b + a


def dot(a, b):
    return jnp.dot(a, b, preferred_element_type=F32)


def dot_cols(a, b):
    return lax.dot_general(a, b, (((1,), (1,)), ((), ())), preferred_element_type=F32)


def dot_rows(a, b):
    return lax.dot_general(a, b, (((0,), (0,)), ((), ())), preferred_element_type=F32)


def gates(pre):
    return jnp.tanh(pre[:, :CH]), 0.5 * jnp.tanh(0.5 * pre[:, CH:]) + 0.5


def forward_local_kernel(local, cw, ow, stream, gated0, slope_f, slope_g, skip):
    for r, size in ((D0, D0), (2 * D0, TILE)):
        at = slice(r - D0, r - D0 + size)
        now = local[r : r + size, :]
        pre = dot(local[at, :], cw[0, :CH, :]) + dot(now, cw[0, CH:, :])
        f, g = gates(pre)
        gated = (f * g).astype(BF16)
        stream[at, :] = (now.astype(F32) + dot(gated, ow[0, :, :CH])).astype(BF16)
        gated0[at, :] = gated
        slope_f[at, :] = (1.0 - f * f) * g
        slope_g[at, :] = f * g * (1.0 - g)
        skip[at, :] = dot(gated, ow[0, :, CH:])


def layer_1(r, stream1, cw, ow, rc, sc, gated1, pre1):
    at = slice(r, r + TILE)
    pre = dot(stream1[at, :], cw[1, :CH, :]) + dot(stream1[r + D1 : r + D1 + TILE, :], cw[1, CH:, :])
    f, g = gates(pre)
    gated = (f * g).astype(BF16)
    gated1[...] = gated
    more = dot(gated, ow[1, :, CH:])
    gc = dot_cols(rc[at, :], ow[1, :, :CH]) + dot_cols(sc[at, :], ow[1, :, CH:])
    pre1[:, :CH] = (gc * ((1.0 - f * f) * g)).astype(BF16)
    pre1[:, CH:] = (gc * (f * g * (1.0 - g))).astype(BF16)
    pc = pre1[...]
    flow = rc[at, :].astype(F32) + dot_cols(pc, cw[1, CH:, :])
    return more, flow, dot_cols(pc, cw[1, :CH, :])


def forward_low_kernel(
    halo, local, cw, ow, rc, sc, stream_high, skip_high,
    early, flow, pre1, stream1, gated0, gated1, slope_f, slope_g, skip,
    ext, skip_low,
):
    ext[:HALO, :] = halo[...]
    ext[HALO:, :] = local[:D0, :]
    for r, size in ((0, TILE), (D1, D0)):
        now = ext[D0 + r : D0 + r + size, :]
        pre = dot(ext[r : r + size, :], cw[0, :CH, :]) + dot(now, cw[0, CH:, :])
        f, g = gates(pre)
        gated = (f * g).astype(BF16)
        stream1[r : r + size, :] = (now.astype(F32) + dot(gated, ow[0, :, :CH])).astype(BF16)
        if r == D1:
            gated0[...] = gated
            slope_f[...] = (1.0 - f * f) * g
            slope_g[...] = f * g * (1.0 - g)
            skip_low[...] = dot(gated, ow[0, :, CH:])
    stream1[HALO:, :] = stream_high[...]
    more, flow[...], ahead = layer_1(0, stream1, cw, ow, rc, sc, gated1, pre1)
    early[...] = ahead.astype(BF16)
    skip[:D0, :] = (skip_low[...] + more[:D0, :]).astype(BF16)
    skip[D0:, :] = (skip_high[:D0, :] + more[D0:, :]).astype(BF16)


def forward_high_kernel(
    stream1, cw, ow, rc, sc, skip_high, skip_low, gated_low, pre_low, flow_before,
    flow_low, flow_high, pre1, gated1, skip,
):
    high = pl.ds(TILE, TILE)
    more, flow_high[...], ahead = layer_1(
        TILE, stream1, cw, ow, rc, sc, gated1.at[high, :], pre1.at[high, :]
    )
    flow_low[...] = flow_before[...] + ahead
    skip[:TILE, :] = skip_low[...]
    skip[TILE:, :] = (skip_high[D0:, :] + more).astype(BF16)
    gated1[:TILE, :] = gated_low[...]
    pre1[:TILE, :] = pre_low[...]


def backward_low_kernel(flow1, low_f, low_g, high_f, high_g, sc, ow, cw, proj, pre0, flow, early):
    fl = flow1[...]
    flow_b = fl.astype(BF16)
    proj[...] = flow_b
    gc = dot_cols(flow_b, ow[0, :, :CH]) + dot_cols(sc[:TILE, :], ow[0, :, CH:])
    pre0[:D0, :CH] = (gc[:D0] * low_f[...]).astype(BF16)
    pre0[:D0, CH:] = (gc[:D0] * low_g[...]).astype(BF16)
    pre0[D0:, :CH] = (gc[D0:] * high_f[:D0, :]).astype(BF16)
    pre0[D0:, CH:] = (gc[D0:] * high_g[:D0, :]).astype(BF16)
    pc = pre0[...]
    flow[...] = fl + dot_cols(pc, cw[0, CH:, :])
    ahead = dot_cols(pc, cw[0, :CH, :])
    early[...] = ahead[:D0, :].astype(BF16)
    flow[:D0, :] += ahead[D0:, :]


def backward_high_kernel(flow1, returned, high_f, high_g, sc, ow, cw, flow_low, proj, pre0, resid, tail):
    fl = flow1[...] + returned[...].astype(F32)
    flow_b = fl.astype(BF16)
    proj[...] = flow_b
    gc = dot_cols(flow_b, ow[0, :, :CH]) + dot_cols(sc[TILE:, :], ow[0, :, CH:])
    pre0[:, :CH] = (gc * high_f[D0:, :]).astype(BF16)
    pre0[:, CH:] = (gc * high_g[D0:, :]).astype(BF16)
    pc = pre0[...]
    fl = fl + dot_cols(pc, cw[0, CH:, :])
    ahead = dot_cols(pc, cw[0, :CH, :])
    resid[:D0, :] = flow_low[:D0, :].astype(BF16)
    resid[D0:TILE, :] = (flow_low[D0:, :] + ahead[:D0, :]).astype(BF16)
    resid[TILE:, :] = (fl[:D0, :] + ahead[D0:, :]).astype(BF16)
    tail[...] = fl[D0:, :]


def place(layer, half, y, z):
    order = Z_ORDERS[half] if layer == 1 else Z_ORDER
    unit, t = divmod(order.index(z), 2)
    if layer == 1:
        return (unit, ring_place(y, 0)), t
    return (ring_place(y, half), unit), t


def gradient_body(core, layer, stream, gated, pre, left, right, mine, other):
    delay = D1 if layer == 1 else D0
    odd = jnp.full((16, CH // 2), core[0], jnp.int32) == 1
    odd_8 = jnp.full((8, CH // 2), core[0], jnp.int32) == 1
    for n in range(4):
        half = n // 2
        cols = slice((n % 2) * 256, (n % 2) * 256 + 256)
        cot = pre[:, n * 256 : (n + 1) * 256]
        for m in range(4):
            start = 0 if m < 2 else delay
            lhs = stream[start : start + ROWS, (m % 2) * 256 : (m % 2) * 256 + 256]
            g = dot_rows(lhs, cot)
            for dz in range(2):
                for y in range(Y):
                    row = dz * 128 + y * 32
                    where, t = place(layer, half, y, m * 2 + dz)
                    at = (half, *where, slice(t * 16, t * 16 + 16), cols)
                    even, uneven = g[row : row + 16], g[row + 16 : row + 32]
                    mine[at] = jnp.where(odd, uneven, even).astype(BF16)
                    other[at] = jnp.where(odd, even, uneven).astype(BF16)
        side = left if n < 2 else right
        g = dot_rows(gated[...], side[:, cols])
        order = Z_ORDERS[half] if layer == 1 else Z_ORDER
        for unit in range(4):
            for y in range(Y):
                where, _ = place(layer, half, y, order[2 * unit])
                at = (half, *where, slice(32, 48), cols)
                mine_parts, other_parts = [], []
                for t in range(2):
                    row = order[unit * 2 + t] * 64 + y * 16
                    even, uneven = g[row : row + 8], g[row + 8 : row + 16]
                    mine_parts.append(jnp.where(odd_8, uneven, even))
                    other_parts.append(jnp.where(odd_8, even, uneven))
                mine[at] = jnp.concatenate(mine_parts, axis=0).astype(BF16)
                other[at] = jnp.concatenate(other_parts, axis=0).astype(BF16)


def gradient_1_kernel(core, stream, gated, pre, left, right, mine, other):
    gradient_body(core, 1, stream, gated, pre, left, right, mine, other)


def gradient_0_kernel(
    core, halo, local, gated_low, gated_high, pre_low, pre_high, left_low, left_high, right,
    mine, other,
    stream, gated, pre, left,
):
    stream[:D0, :] = halo[D1:, :]
    stream[D0:, :] = local[...]
    gated[:D0, :] = gated_low[...]
    gated[D0:, :] = gated_high[...]
    pre[:TILE, :] = pre_low[...]
    pre[TILE:, :] = pre_high[...]
    left[:TILE, :] = left_low[...]
    left[TILE:, :] = left_high[...]
    gradient_body(core, 0, stream, gated, pre, left, right, mine, other)


def kernel_call(kernel, shapes, args, flops, moved, limit, scratch=(), smem=0):
    vmem = pl.BlockSpec(memory_space=pltpu.VMEM)
    return pl.pallas_call(
        kernel,
        out_shape=[jax.ShapeDtypeStruct(s, t) for s, t in shapes],
        in_specs=[pl.BlockSpec(memory_space=pltpu.SMEM)] * smem + [vmem] * (len(args) - smem),
        out_specs=[vmem] * len(shapes),
        scratch_shapes=scratch,
        compiler_params=pltpu.CompilerParams(vmem_limit_bytes=limit * MIB),
        cost_estimate=pl.CostEstimate(flops=flops, bytes_accessed=moved, transcendentals=0),
    )(*args)


def halve(parts, axis, pairs, bit):
    kept = lax.dynamic_index_in_dim(parts, bit, 0, False, allow_negative_indices=False)
    sent = lax.dynamic_index_in_dim(parts, 1 - bit, 0, False, allow_negative_indices=False)
    got = lax.ppermute(sent, axis, list(enumerate(pairs)))
    return (kept.astype(F32) + got.astype(F32)).astype(BF16)


def picked(parts, i):
    return lax.dynamic_index_in_dim(parts, i, 0, False, allow_negative_indices=False)


def halve_of_two(terms, axis, pairs, bit):
    sent = sum(picked(t, 1 - bit).astype(F32) for t in terms).astype(BF16)
    got = lax.ppermute(sent, axis, list(enumerate(pairs)))
    return (sum(picked(t, bit).astype(F32) for t in terms) + got.astype(F32)).astype(BF16)


def split(s):
    return s.reshape((2, 2) + s.shape[1:])


def split_last(s):
    lead = s.shape[:-2]
    conv, out = s[..., :32, :].reshape(*lead, 2, 16, CH), s[..., 32:, :].reshape(*lead, 2, 8, CH)
    return jnp.moveaxis(jnp.concatenate([conv, out], axis=-2), -3, 0)


def together(a, b):
    return lax.optimization_barrier((a, b))


def from_x(s):
    return [lax.ppermute(s, "x", [(i, (i + k) % X) for i in range(X)]) for k in (2, 1, 3)]


def along(value, steps):
    initial, last = (max(0, -steps), min(X, X - steps))
    return lax.ppermute(value, "x", [(s, s + steps) for s in range(initial, last)])


def assemble_kernel(own, opposite, one, two, conv, out):
    for layer in range(2):
        for half in range(2):
            i = 2 * layer + half
            at = slice(half * CH, half * CH + CH)
            piece = (own[i].astype(F32) + opposite[i].astype(F32)) + (one[i].astype(F32) + two[i].astype(F32))
            conv[layer, :, at] = piece[:16]
            out[layer, :, at] = piece[16:]


def ring_bits(i):
    b = i >> 1
    return (i + b) & 1, b


def on_device(resid_in, conv_weight, out_weight, resid_cot, skip_cot):
    x0, rc, sc = resid_in[0], resid_cot[0], skip_cot[0]
    core = lax.axis_index("c")[None]
    yi, zi = lax.axis_index("y"), lax.axis_index("z")
    ya, yb = ring_bits(yi)
    z_bits = [(((i + 1) >> 1) & 1, (Z_SECOND >> i) & 1, (Z_THIRD >> i) & 1) for i in (zi, (zi - 1) & (Z - 1))]
    high = ROWS - D0
    halo = along(x0[ROWS - HALO :], 1)
    stream_high, gated_high, high_f, high_g, skip_high = kernel_call(
        forward_local_kernel,
        [((high, CH), BF16)] * 2 + [((high, CH), F32)] * 3,
        (x0, conv_weight, out_weight),
        12 * 10**8,
        10**7,
        16,
    )
    halo, high_f = lax.optimization_barrier((halo, high_f))
    early1, flow_before, pre1_low, stream1, gated_low, gated1_low, low_f, low_g, skip_low = kernel_call(
        forward_low_kernel,
        [((D1, CH), BF16), ((TILE, CH), F32), ((TILE, 2 * CH), BF16), ((ROWS + D1, CH), BF16)]
        + [((D0, CH), BF16), ((TILE, CH), BF16)]
        + [((D0, CH), F32)] * 2
        + [((TILE, CH), BF16)],
        (halo, x0, conv_weight, out_weight, rc, sc, stream_high, skip_high),
        2 * 10**9,
        10**7,
        16,
        [pltpu.VMEM((HALO + D0, CH), BF16), pltpu.VMEM((D0, CH), F32)],
    )
    returned1 = along(early1, -1)
    flow1_low, flow1_high, pre1, gated1, skip = kernel_call(
        forward_high_kernel,
        [((TILE, CH), F32)] * 2 + [((ROWS, 2 * CH), BF16), ((ROWS, CH), BF16), ((ROWS, CH), BF16)],
        (stream1, conv_weight, out_weight, rc, sc, skip_high, skip_low, gated1_low, pre1_low, flow_before),
        5 * 10**9,
        10**7,
        16,
    )
    pieces = (4, 4, 48, CH)
    mine1, other1 = kernel_call(
        gradient_1_kernel,
        [((2,) + pieces, BF16)] * 2,
        (core, stream1, gated1, pre1, rc, sc),
        5 * 10**9,
        6 * 10**6,
        16,
        smem=1,
    )
    proj_low, pre_low, flow_low, early0 = kernel_call(
        backward_low_kernel,
        [((TILE, CH), BF16), ((TILE, 2 * CH), BF16), ((TILE, CH), F32), ((D0, CH), BF16)],
        (flow1_low, low_f, low_g, high_f, high_g, sc, out_weight, conv_weight),
        25 * 10**8,
        6 * 10**6,
        16,
    )
    returned1, mine1, other1, flow_low = lax.optimization_barrier((returned1, mine1, other1, flow_low))
    returned0 = along(early0, -1)
    proj_high, pre_high, resid_most, tail = kernel_call(
        backward_high_kernel,
        [((TILE, CH), BF16), ((TILE, 2 * CH), BF16), ((high, CH), BF16), ((D0, CH), F32)],
        (flow1_high, returned1, high_f, high_g, sc, out_weight, conv_weight, flow_low),
        25 * 10**8,
        6 * 10**6,
        16,
    )
    got1 = lax.ppermute(other1, "c", [(0, 1), (1, 0)])
    mine0, other0 = kernel_call(
        gradient_0_kernel,
        [((2,) + pieces, BF16)] * 2,
        (core, halo, x0, gated_low, gated_high, pre_low, pre_high, proj_low, proj_high, sc),
        5 * 10**9,
        6 * 10**6,
        16,
        [pltpu.VMEM((ROWS + D0, CH), BF16), pltpu.VMEM((ROWS, CH), BF16)]
        + [pltpu.VMEM((ROWS, 2 * CH), BF16), pltpu.VMEM((ROWS, CH), BF16)],
        smem=1,
    )
    got0 = lax.ppermute(other0, "c", [(0, 1), (1, 0)])
    resid = jnp.concatenate([resid_most, (tail + returned0.astype(F32)).astype(BF16)])

    pairs_1 = (Z_PAIRS, Z_PAIRS_NEXT)
    y_steps = ((FIRST, ya), (SECOND, yb))
    s1 = [
        halve_of_two((split(mine1[half]), split(got1[half])), "z", pairs_1[half][0], z_bits[half][0])
        for half in range(2)
    ]
    s0 = [halve_of_two((split(mine0[half]), split(got0[half])), "y", *y_steps[half]) for half in range(2)]
    s0, s1 = together(s0, s1)
    s0 = [halve(s0[half], "y", *y_steps[1 - half]) for half in range(2)]
    s1 = [halve(s1[half], "z", pairs_1[half][1], z_bits[half][1]) for half in range(2)]
    s0, s1 = together(s0, s1)
    s0 = halve(split(jnp.stack(s0, axis=1)), "z", Z_PAIRS[0], z_bits[0][0])
    s1 = halve(split(jnp.stack(s1, axis=1)), "y", *y_steps[0])
    s0, s1 = together(s0, s1)
    s0 = halve(s0, "z", Z_PAIRS[1], z_bits[0][1])
    s1 = halve(s1, "y", *y_steps[1])
    most, least = together(jnp.concatenate([s0, s1[:1]]), s1[1:])
    most = halve(split_last(most), "z", Z_PAIRS[2], z_bits[0][2])
    least = halve(split_last(least), "z", Z_PAIRS_NEXT[2], z_bits[1][2])
    s = jnp.concatenate([most, least])
    conv_grad, out_grad = kernel_call(
        assemble_kernel,
        [((2, 16, 1024), F32), ((2, 8, 1024), F32)],
        [s] + from_x(s),
        10**6,
        10**6,
        8,
    )
    return conv_grad, out_grad, resid[None], skip[None]


def solution(mesh):
    fine = Mesh(mesh.devices.reshape(Z, Y, CORES, X), ("z", "y", "c", "x"))
    dp = ("z", "y", "c")
    return jax.shard_map(
        on_device,
        mesh=fine,
        in_specs=(P(dp, "x", None), P(), P(), P(dp, "x", None), P(dp, "x", None)),
        out_specs=(P(None, dp, None), P(None, dp, None), P(dp, "x", None), P(dp, "x", None)),
        check_vma=False,
    )
```

```python
import functools

import jax
import jax.numpy as jnp
from jax import lax
from jax.experimental import pallas as pl
from jax.experimental.pallas import tpu as pltpu
from jax.sharding import Mesh, PartitionSpec as P

F32, BF16 = jnp.float32, jnp.bfloat16
Z, Y, CORES, X = 8, 4, 2, 4
D0, D1 = 128, 256
ROWS, CH = 512, 512
HALO = D0 + D1
TILE = 256
MIB = 1024 * 1024

FIRST, SECOND = (1, 0, 3, 2), (3, 2, 1, 0)
BIT_A, BIT_B = (0, 1, 1, 0), (0, 0, 1, 1)
Z_PAIRS = ((1, 0, 3, 2, 5, 4, 7, 6), (7, 2, 1, 4, 3, 6, 5, 0), (3, 6, 5, 0, 7, 2, 1, 4))
Z_ORDER = (0, 3, 7, 4, 1, 6, 2, 5)
Z_ORDERS = (Z_ORDER, tuple((i + 1) % Z for i in Z_ORDER))
Z_PAIRS_NEXT = tuple(tuple((pairs[(i - 1) % Z] + 1) % Z for i in range(Z)) for pairs in Z_PAIRS)
Z_SECOND, Z_THIRD = (sum(((Z_ORDER.index(i) >> k) & 1) << i for i in range(Z)) for k in (1, 0))


def ring_place(i, half):
    a, b = BIT_A[i], BIT_B[i]
    return 2 * a + b if half == 0 else 2 * b + a


def dot(a, b):
    return jnp.dot(a, b, preferred_element_type=F32)


def dot_cols(a, b):
    return lax.dot_general(a, b, (((1,), (1,)), ((), ())), preferred_element_type=F32)


def dot_rows(a, b):
    return lax.dot_general(a, b, (((0,), (0,)), ((), ())), preferred_element_type=F32)


def gates(pre):
    return jnp.tanh(pre[:, :CH]), 0.5 * jnp.tanh(0.5 * pre[:, CH:]) + 0.5


def forward_local_kernel(local, cw, ow, stream, gated0, slope_f, slope_g, skip):
    for r, size in ((D0, D0), (2 * D0, TILE)):
        at = slice(r - D0, r - D0 + size)
        now = local[r : r + size, :]
        pre = dot(local[at, :], cw[0, :CH, :]) + dot(now, cw[0, CH:, :])
        f, g = gates(pre)
        gated = (f * g).astype(BF16)
        stream[at, :] = (now.astype(F32) + dot(gated, ow[0, :, :CH])).astype(BF16)
        gated0[at, :] = gated
        slope_f[at, :] = (1.0 - f * f) * g
        slope_g[at, :] = f * g * (1.0 - g)
        skip[at, :] = dot(gated, ow[0, :, CH:])


def layer_1(r, stream1, cw, ow, rc, sc, gated1, pre1):
    at = slice(r, r + TILE)
    pre = dot(stream1[at, :], cw[1, :CH, :]) + dot(stream1[r + D1 : r + D1 + TILE, :], cw[1, CH:, :])
    f, g = gates(pre)
    gated = (f * g).astype(BF16)
    gated1[...] = gated
    gc = dot_cols(rc[at, :], ow[1, :, :CH]) + dot_cols(sc[at, :], ow[1, :, CH:])
    pre1[:, :CH] = (gc * ((1.0 - f * f) * g)).astype(BF16)
    pre1[:, CH:] = (gc * (f * g * (1.0 - g))).astype(BF16)
    return dot_cols(pre1[...], cw[1, :CH, :])


def forward_low_kernel(
    halo, local, cw, ow, rc, sc, stream_high,
    early, pre1, stream1, gated0, gated1, slope_f, slope_g,
    ext,
):
    ext[:HALO, :] = halo[...]
    ext[HALO:, :] = local[:D0, :]
    for r, size in ((0, TILE), (D1, D0)):
        now = ext[D0 + r : D0 + r + size, :]
        pre = dot(ext[r : r + size, :], cw[0, :CH, :]) + dot(now, cw[0, CH:, :])
        f, g = gates(pre)
        gated = (f * g).astype(BF16)
        stream1[r : r + size, :] = (now.astype(F32) + dot(gated, ow[0, :, :CH])).astype(BF16)
        if r == D1:
            gated0[...] = gated
            slope_f[...] = (1.0 - f * f) * g
            slope_g[...] = f * g * (1.0 - g)
    stream1[HALO:, :] = stream_high[...]
    early[...] = layer_1(0, stream1, cw, ow, rc, sc, gated1, pre1).astype(BF16)


def forward_high_kernel(
    stream1, cw, ow, rc, sc, skip_high, gated0_low, gated_low, pre_low,
    flow_low, flow_high, pre1, gated1, skip,
):
    high = pl.ds(TILE, TILE)
    ahead = layer_1(TILE, stream1, cw, ow, rc, sc, gated1.at[high, :], pre1.at[high, :])
    gated1[:TILE, :] = gated_low[...]
    pre1[:TILE, :] = pre_low[...]
    flow_high[...] = rc[TILE:, :].astype(F32) + dot_cols(pre1[TILE:, :], cw[1, CH:, :])
    flow_low[...] = rc[:TILE, :].astype(F32) + dot_cols(pre_low[...], cw[1, CH:, :]) + ahead
    more = dot(gated1[...], ow[1, :, CH:])
    skip[:D0, :] = (dot(gated0_low[...], ow[0, :, CH:]) + more[:D0, :]).astype(BF16)
    skip[D0:, :] = (skip_high[...] + more[D0:, :]).astype(BF16)


def backward_low_kernel(flow1, low_f, low_g, high_f, high_g, sc, ow, cw, proj, pre0, flow, early):
    fl = flow1[...]
    flow_b = fl.astype(BF16)
    proj[...] = flow_b
    gc = dot_cols(flow_b, ow[0, :, :CH]) + dot_cols(sc[:TILE, :], ow[0, :, CH:])
    pre0[:D0, :CH] = (gc[:D0] * low_f[...]).astype(BF16)
    pre0[:D0, CH:] = (gc[:D0] * low_g[...]).astype(BF16)
    pre0[D0:, :CH] = (gc[D0:] * high_f[:D0, :]).astype(BF16)
    pre0[D0:, CH:] = (gc[D0:] * high_g[:D0, :]).astype(BF16)
    pc = pre0[...]
    flow[...] = fl + dot_cols(pc, cw[0, CH:, :])
    ahead = dot_cols(pc, cw[0, :CH, :])
    early[...] = ahead[:D0, :].astype(BF16)
    flow[:D0, :] += ahead[D0:, :]


def backward_high_kernel(flow1, returned, high_f, high_g, sc, ow, cw, flow_low, proj, pre0, resid, tail):
    fl = flow1[...] + returned[...].astype(F32)
    flow_b = fl.astype(BF16)
    proj[...] = flow_b
    gc = dot_cols(flow_b, ow[0, :, :CH]) + dot_cols(sc[TILE:, :], ow[0, :, CH:])
    pre0[:, :CH] = (gc * high_f[D0:, :]).astype(BF16)
    pre0[:, CH:] = (gc * high_g[D0:, :]).astype(BF16)
    pc = pre0[...]
    fl = fl + dot_cols(pc, cw[0, CH:, :])
    ahead = dot_cols(pc, cw[0, :CH, :])
    resid[:D0, :] = flow_low[:D0, :].astype(BF16)
    resid[D0:TILE, :] = (flow_low[D0:, :] + ahead[:D0, :]).astype(BF16)
    resid[TILE:, :] = (fl[:D0, :] + ahead[D0:, :]).astype(BF16)
    tail[...] = fl[D0:, :]


def place(layer, half, y, z):
    order = Z_ORDERS[half] if layer == 1 else Z_ORDER
    unit, t = divmod(order.index(z), 2)
    if layer == 1:
        return (unit, ring_place(y, 0)), t
    return (ring_place(y, half), unit), t


def gradient_body(core, layer, stream, gated, pre, left, right, mine, sent, other, sems):
    delay = D1 if layer == 1 else D0
    copies = [pltpu.make_async_copy(other.at[half], sent.at[half], sems.at[half]) for half in range(2)]
    odd = jnp.full((16, CH // 2), core[0], jnp.int32) == 1
    odd_8 = jnp.full((8, CH // 2), core[0], jnp.int32) == 1
    for n in range(4):
        half = n // 2
        cols = slice((n % 2) * 256, (n % 2) * 256 + 256)
        cot = pre[:, n * 256 : (n + 1) * 256]
        for m in range(4):
            start = 0 if m < 2 else delay
            lhs = stream[start : start + ROWS, (m % 2) * 256 : (m % 2) * 256 + 256]
            g = dot_rows(lhs, cot)
            for dz in range(2):
                for y in range(Y):
                    row = dz * 128 + y * 32
                    where, t = place(layer, half, y, m * 2 + dz)
                    at = (half, *where, slice(t * 16, t * 16 + 16), cols)
                    even, uneven = g[row : row + 16], g[row + 16 : row + 32]
                    mine[at] = jnp.where(odd, uneven, even).astype(BF16)
                    other[at] = jnp.where(odd, even, uneven).astype(BF16)
        side = left if n < 2 else right
        g = dot_rows(gated[...], side[:, cols])
        order = Z_ORDERS[half] if layer == 1 else Z_ORDER
        for unit in range(4):
            for y in range(Y):
                where, _ = place(layer, half, y, order[2 * unit])
                at = (half, *where, slice(32, 48), cols)
                mine_parts, other_parts = [], []
                for t in range(2):
                    row = order[unit * 2 + t] * 64 + y * 16
                    even, uneven = g[row : row + 8], g[row + 8 : row + 16]
                    mine_parts.append(jnp.where(odd_8, uneven, even))
                    other_parts.append(jnp.where(odd_8, even, uneven))
                mine[at] = jnp.concatenate(mine_parts, axis=0).astype(BF16)
                other[at] = jnp.concatenate(other_parts, axis=0).astype(BF16)
        if n % 2 == 1:
            copies[half].start()
    for copy in copies:
        copy.wait()


def gradient_1_kernel(core, *refs):
    gradient_body(core, 1, *refs)


def gradient_0_kernel(
    core, halo, local, gated_low, gated_high, pre_low, pre_high, left_low, left_high, right,
    mine, sent,
    stream, gated, pre, left, other, sems,
):
    stream[:D0, :] = halo[D1:, :]
    stream[D0:, :] = local[...]
    gated[:D0, :] = gated_low[...]
    gated[D0:, :] = gated_high[...]
    pre[:TILE, :] = pre_low[...]
    pre[TILE:, :] = pre_high[...]
    left[:TILE, :] = left_low[...]
    left[TILE:, :] = left_high[...]
    gradient_body(core, 0, stream, gated, pre, left, right, mine, sent, other, sems)


def kernel_call(kernel, shapes, args, flops, moved, limit, scratch=(), smem=0, sent=0):
    vmem = pl.BlockSpec(memory_space=pltpu.VMEM)
    return pl.pallas_call(
        kernel,
        out_shape=[jax.ShapeDtypeStruct(s, t) for s, t in shapes],
        in_specs=[pl.BlockSpec(memory_space=pltpu.SMEM)] * smem + [vmem] * (len(args) - smem),
        out_specs=[vmem] * (len(shapes) - sent) + [pl.BlockSpec(memory_space=pl.ANY)] * sent,
        scratch_shapes=scratch,
        compiler_params=pltpu.CompilerParams(vmem_limit_bytes=limit * MIB),
        cost_estimate=pl.CostEstimate(flops=flops, bytes_accessed=moved, transcendentals=0),
    )(*args)


def halve(parts, axis, pairs, bit):
    kept = lax.dynamic_index_in_dim(parts, bit, 0, False, allow_negative_indices=False)
    sent = lax.dynamic_index_in_dim(parts, 1 - bit, 0, False, allow_negative_indices=False)
    got = lax.ppermute(sent, axis, list(enumerate(pairs)))
    return (kept.astype(F32) + got.astype(F32)).astype(BF16)


def picked(parts, i):
    return lax.dynamic_index_in_dim(parts, i, 0, False, allow_negative_indices=False)


def halve_of_two(terms, axis, pairs, bit):
    sent = sum(picked(t, 1 - bit).astype(F32) for t in terms).astype(BF16)
    got = lax.ppermute(sent, axis, list(enumerate(pairs)))
    return (sum(picked(t, bit).astype(F32) for t in terms) + got.astype(F32)).astype(BF16)


def split(s):
    return s.reshape((2, 2) + s.shape[1:])


def split_last(s):
    lead = s.shape[:-2]
    conv, out = s[..., :32, :].reshape(*lead, 2, 16, CH), s[..., 32:, :].reshape(*lead, 2, 8, CH)
    return jnp.moveaxis(jnp.concatenate([conv, out], axis=-2), -3, 0)


def together(a, b):
    return lax.optimization_barrier((a, b))


def from_x(s):
    return [lax.ppermute(s, "x", [(i, (i + k) % X) for i in range(X)]) for k in (2, 1, 3)]


def along(value, steps):
    initial, last = (max(0, -steps), min(X, X - steps))
    return lax.ppermute(value, "x", [(s, s + steps) for s in range(initial, last)])


def assemble_kernel(own, opposite, one, two, conv, out):
    for layer in range(2):
        for half in range(2):
            i = 2 * layer + half
            at = slice(half * CH, half * CH + CH)
            piece = (own[i].astype(F32) + opposite[i].astype(F32)) + (one[i].astype(F32) + two[i].astype(F32))
            conv[layer, :, at] = piece[:16]
            out[layer, :, at] = piece[16:]


def ring_bits(i):
    b = i >> 1
    return (i + b) & 1, b


def on_device(resid_in, conv_weight, out_weight, resid_cot, skip_cot):
    x0, rc, sc = resid_in[0], resid_cot[0], skip_cot[0]
    core = lax.axis_index("c")[None]
    yi, zi = lax.axis_index("y"), lax.axis_index("z")
    ya, yb = ring_bits(yi)
    z_bits = [(((i + 1) >> 1) & 1, (Z_SECOND >> i) & 1, (Z_THIRD >> i) & 1) for i in (zi, (zi - 1) & (Z - 1))]
    high = ROWS - D0
    halo = along(x0[ROWS - HALO :], 1)
    stream_high, gated_high, high_f, high_g, skip_high = kernel_call(
        forward_local_kernel,
        [((high, CH), BF16)] * 2 + [((high, CH), F32)] * 3,
        (x0, conv_weight, out_weight),
        12 * 10**8,
        10**7,
        16,
    )
    halo, high_f = lax.optimization_barrier((halo, high_f))
    early1, pre1_low, stream1, gated_low, gated1_low, low_f, low_g = kernel_call(
        forward_low_kernel,
        [((D1, CH), BF16), ((TILE, 2 * CH), BF16), ((ROWS + D1, CH), BF16)]
        + [((D0, CH), BF16), ((TILE, CH), BF16)]
        + [((D0, CH), F32)] * 2,
        (halo, x0, conv_weight, out_weight, rc, sc, stream_high),
        2 * 10**9,
        10**7,
        16,
        [pltpu.VMEM((HALO + D0, CH), BF16)],
    )
    returned1 = along(early1, -1)
    flow1_low, flow1_high, pre1, gated1, skip = kernel_call(
        forward_high_kernel,
        [((TILE, CH), F32)] * 2 + [((ROWS, 2 * CH), BF16), ((ROWS, CH), BF16), ((ROWS, CH), BF16)],
        (stream1, conv_weight, out_weight, rc, sc, skip_high, gated_low, gated1_low, pre1_low),
        5 * 10**9,
        10**7,
        16,
    )
    pieces = (4, 4, 48, CH)
    own_copy = [pltpu.VMEM((2,) + pieces, BF16), pltpu.SemaphoreType.DMA((2,))]
    mine1, other1 = kernel_call(
        gradient_1_kernel,
        [((2,) + pieces, BF16)] * 2,
        (core, stream1, gated1, pre1, rc, sc),
        5 * 10**9,
        6 * 10**6,
        16,
        own_copy,
        smem=1,
        sent=1,
    )
    proj_low, pre_low, flow_low, early0 = kernel_call(
        backward_low_kernel,
        [((TILE, CH), BF16), ((TILE, 2 * CH), BF16), ((TILE, CH), F32), ((D0, CH), BF16)],
        (flow1_low, low_f, low_g, high_f, high_g, sc, out_weight, conv_weight),
        25 * 10**8,
        6 * 10**6,
        16,
    )
    returned1, mine1, flow_low = lax.optimization_barrier((returned1, mine1, flow_low))
    returned0 = along(early0, -1)
    proj_high, pre_high, resid_most, tail = kernel_call(
        backward_high_kernel,
        [((TILE, CH), BF16), ((TILE, 2 * CH), BF16), ((high, CH), BF16), ((D0, CH), F32)],
        (flow1_high, returned1, high_f, high_g, sc, out_weight, conv_weight, flow_low),
        25 * 10**8,
        6 * 10**6,
        16,
    )
    got1 = lax.ppermute(other1, "c", [(0, 1), (1, 0)])
    mine0, other0 = kernel_call(
        gradient_0_kernel,
        [((2,) + pieces, BF16)] * 2,
        (core, halo, x0, gated_low, gated_high, pre_low, pre_high, proj_low, proj_high, sc),
        5 * 10**9,
        6 * 10**6,
        16,
        [pltpu.VMEM((ROWS + D0, CH), BF16), pltpu.VMEM((ROWS, CH), BF16)]
        + [pltpu.VMEM((ROWS, 2 * CH), BF16), pltpu.VMEM((ROWS, CH), BF16)]
        + own_copy,
        smem=1,
        sent=1,
    )
    got0 = lax.ppermute(other0, "c", [(0, 1), (1, 0)])
    resid = jnp.concatenate([resid_most, (tail + returned0.astype(F32)).astype(BF16)])

    pairs_1 = (Z_PAIRS, Z_PAIRS_NEXT)
    y_steps = ((FIRST, ya), (SECOND, yb))
    s1 = [
        halve_of_two((split(mine1[half]), split(got1[half])), "z", pairs_1[half][0], z_bits[half][0])
        for half in range(2)
    ]
    s0 = [halve_of_two((split(mine0[half]), split(got0[half])), "y", *y_steps[half]) for half in range(2)]
    s0, s1 = together(s0, s1)
    s0 = [halve(s0[half], "y", *y_steps[1 - half]) for half in range(2)]
    s1 = [halve(s1[half], "z", pairs_1[half][1], z_bits[half][1]) for half in range(2)]
    s0, s1 = together(s0, s1)
    s0 = halve(split(jnp.stack(s0, axis=1)), "z", Z_PAIRS[0], z_bits[0][0])
    s1 = halve(split(jnp.stack(s1, axis=1)), "y", *y_steps[0])
    s0, s1 = together(s0, s1)
    s0 = halve(s0, "z", Z_PAIRS[1], z_bits[0][1])
    s1 = halve(s1, "y", *y_steps[1])
    most, least = together(jnp.concatenate([s0, s1[:1]]), s1[1:])
    most = halve(split_last(most), "z", Z_PAIRS[2], z_bits[0][2])
    least = halve(split_last(least), "z", Z_PAIRS_NEXT[2], z_bits[1][2])
    s = jnp.concatenate([most, least])
    conv_grad, out_grad = kernel_call(
        assemble_kernel,
        [((2, 16, 1024), F32), ((2, 8, 1024), F32)],
        [s] + from_x(s),
        10**6,
        10**6,
        8,
    )
    return conv_grad, out_grad, resid[None], skip[None]


def solution(mesh):
    fine = Mesh(mesh.devices.reshape(Z, Y, CORES, X), ("z", "y", "c", "x"))
    dp = ("z", "y", "c")
    return jax.shard_map(
        on_device,
        mesh=fine,
        in_specs=(P(dp, "x", None), P(), P(), P(dp, "x", None), P(dp, "x", None)),
        out_specs=(P(None, dp, None), P(None, dp, None), P(dp, "x", None), P(dp, "x", None)),
        check_vma=False,
    )
```

```python
import functools

import jax
import jax.numpy as jnp
from jax import lax
from jax.experimental import pallas as pl
from jax.experimental.pallas import tpu as pltpu
from jax.sharding import Mesh, PartitionSpec as P

F32, BF16 = jnp.float32, jnp.bfloat16
Z, Y, CORES, X = 8, 4, 2, 4
D0, D1 = 128, 256
ROWS, CH = 512, 512
HALO = D0 + D1
TILE = 256
MIB = 1024 * 1024

FIRST, SECOND = (1, 0, 3, 2), (3, 2, 1, 0)
BIT_A, BIT_B = (0, 1, 1, 0), (0, 0, 1, 1)
Z_PAIRS = ((1, 0, 3, 2, 5, 4, 7, 6), (7, 2, 1, 4, 3, 6, 5, 0), (3, 6, 5, 0, 7, 2, 1, 4))
Z_ORDER = (0, 3, 7, 4, 1, 6, 2, 5)
Z_ORDERS = (Z_ORDER, tuple((i + 1) % Z for i in Z_ORDER))
Z_PAIRS_NEXT = tuple(tuple((pairs[(i - 1) % Z] + 1) % Z for i in range(Z)) for pairs in Z_PAIRS)
Z_SECOND, Z_THIRD = (sum(((Z_ORDER.index(i) >> k) & 1) << i for i in range(Z)) for k in (1, 0))


def ring_place(i, half):
    a, b = BIT_A[i], BIT_B[i]
    return 2 * a + b if half == 0 else 2 * b + a


def dot(a, b):
    return jnp.dot(a, b, preferred_element_type=F32)


def dot_cols(a, b):
    return lax.dot_general(a, b, (((1,), (1,)), ((), ())), preferred_element_type=F32)


def dot_rows(a, b):
    return lax.dot_general(a, b, (((0,), (0,)), ((), ())), preferred_element_type=F32)


def gates(pre):
    return jnp.tanh(pre[:, :CH]), 0.5 * jnp.tanh(0.5 * pre[:, CH:]) + 0.5


def forward_local_kernel(local, cw, ow, stream, gated0, slope_f, slope_g, skip):
    for r, size in ((D0, D0), (2 * D0, TILE)):
        at = slice(r - D0, r - D0 + size)
        now = local[r : r + size, :]
        pre = dot(local[at, :], cw[0, :CH, :]) + dot(now, cw[0, CH:, :])
        f, g = gates(pre)
        gated = (f * g).astype(BF16)
        stream[at, :] = (now.astype(F32) + dot(gated, ow[0, :, :CH])).astype(BF16)
        gated0[at, :] = gated
        slope_f[at, :] = (1.0 - f * f) * g
        slope_g[at, :] = f * g * (1.0 - g)
        skip[at, :] = dot(gated, ow[0, :, CH:])


def layer_1(r, stream1, cw, ow, rc, sc, gated1, pre1):
    at = slice(r, r + TILE)
    pre = dot(stream1[at, :], cw[1, :CH, :]) + dot(stream1[r + D1 : r + D1 + TILE, :], cw[1, CH:, :])
    f, g = gates(pre)
    gated = (f * g).astype(BF16)
    gated1[...] = gated
    gc = dot_cols(rc[at, :], ow[1, :, :CH]) + dot_cols(sc[at, :], ow[1, :, CH:])
    pre1[:, :CH] = (gc * ((1.0 - f * f) * g)).astype(BF16)
    pre1[:, CH:] = (gc * (f * g * (1.0 - g))).astype(BF16)
    return dot_cols(pre1[...], cw[1, :CH, :])


def forward_low_kernel(
    halo, local, cw, ow, rc, sc, stream_high,
    early, pre1, stream1, gated0, gated1, slope_f, slope_g,
    ext,
):
    ext[:HALO, :] = halo[...]
    ext[HALO:, :] = local[:D0, :]
    for r, size in ((0, TILE), (D1, D0)):
        now = ext[D0 + r : D0 + r + size, :]
        pre = dot(ext[r : r + size, :], cw[0, :CH, :]) + dot(now, cw[0, CH:, :])
        f, g = gates(pre)
        gated = (f * g).astype(BF16)
        stream1[r : r + size, :] = (now.astype(F32) + dot(gated, ow[0, :, :CH])).astype(BF16)
        if r == D1:
            gated0[...] = gated
            slope_f[...] = (1.0 - f * f) * g
            slope_g[...] = f * g * (1.0 - g)
    stream1[HALO:, :] = stream_high[...]
    early[...] = layer_1(0, stream1, cw, ow, rc, sc, gated1, pre1).astype(BF16)


def forward_high_kernel(
    stream1, cw, ow, rc, sc, skip_high, gated0_low, gated_low, pre_low,
    flow_low, flow_high, pre1, gated1, skip,
):
    high = pl.ds(TILE, TILE)
    ahead = layer_1(TILE, stream1, cw, ow, rc, sc, gated1.at[high, :], pre1.at[high, :])
    gated1[:TILE, :] = gated_low[...]
    pre1[:TILE, :] = pre_low[...]
    flow_high[...] = rc[TILE:, :].astype(F32) + dot_cols(pre1[TILE:, :], cw[1, CH:, :])
    flow_low[...] = rc[:TILE, :].astype(F32) + dot_cols(pre_low[...], cw[1, CH:, :]) + ahead
    more = dot(gated1[...], ow[1, :, CH:])
    skip[:D0, :] = (dot(gated0_low[...], ow[0, :, CH:]) + more[:D0, :]).astype(BF16)
    skip[D0:, :] = (skip_high[...] + more[D0:, :]).astype(BF16)


def backward_low_kernel(flow1, low_f, low_g, high_f, high_g, sc, ow, cw, proj, pre0, flow, early):
    fl = flow1[...]
    flow_b = fl.astype(BF16)
    proj[...] = flow_b
    gc = dot_cols(flow_b, ow[0, :, :CH]) + dot_cols(sc[:TILE, :], ow[0, :, CH:])
    pre0[:D0, :CH] = (gc[:D0] * low_f[...]).astype(BF16)
    pre0[:D0, CH:] = (gc[:D0] * low_g[...]).astype(BF16)
    pre0[D0:, :CH] = (gc[D0:] * high_f[:D0, :]).astype(BF16)
    pre0[D0:, CH:] = (gc[D0:] * high_g[:D0, :]).astype(BF16)
    pc = pre0[...]
    flow[...] = fl + dot_cols(pc, cw[0, CH:, :])
    ahead = dot_cols(pc, cw[0, :CH, :])
    early[...] = ahead[:D0, :].astype(BF16)
    flow[:D0, :] += ahead[D0:, :]


def backward_high_kernel(flow1, returned, high_f, high_g, sc, ow, cw, flow_low, proj, pre0, resid, tail):
    fl = flow1[...] + returned[...].astype(F32)
    flow_b = fl.astype(BF16)
    proj[...] = flow_b
    gc = dot_cols(flow_b, ow[0, :, :CH]) + dot_cols(sc[TILE:, :], ow[0, :, CH:])
    pre0[:, :CH] = (gc * high_f[D0:, :]).astype(BF16)
    pre0[:, CH:] = (gc * high_g[D0:, :]).astype(BF16)
    pc = pre0[...]
    fl = fl + dot_cols(pc, cw[0, CH:, :])
    ahead = dot_cols(pc, cw[0, :CH, :])
    resid[:D0, :] = flow_low[:D0, :].astype(BF16)
    resid[D0:TILE, :] = (flow_low[D0:, :] + ahead[:D0, :]).astype(BF16)
    resid[TILE:, :] = (fl[:D0, :] + ahead[D0:, :]).astype(BF16)
    tail[...] = fl[D0:, :]


def place(layer, half, y, z):
    order = Z_ORDERS[half] if layer == 1 else Z_ORDER
    unit, t = divmod(order.index(z), 2)
    if layer == 1:
        return (unit, ring_place(y, 0)), t
    return (ring_place(y, half), unit), t


def gradient_body(core, layer, stream, gated, pre, left, right, mine, sent, other, sems):
    delay = D1 if layer == 1 else D0
    copies = [pltpu.make_async_copy(other.at[half], sent.at[half], sems.at[half]) for half in range(2)]
    odd = jnp.full((16, CH // 2), core[0], jnp.int32) == 1
    odd_8 = jnp.full((8, CH // 2), core[0], jnp.int32) == 1
    for n in range(4):
        half = n // 2
        cols = slice((n % 2) * 256, (n % 2) * 256 + 256)
        cot = pre[:, n * 256 : (n + 1) * 256]
        for m in range(4):
            start = 0 if m < 2 else delay
            lhs = stream[start : start + ROWS, (m % 2) * 256 : (m % 2) * 256 + 256]
            g = dot_rows(lhs, cot)
            for dz in range(2):
                for y in range(Y):
                    row = dz * 128 + y * 32
                    where, t = place(layer, half, y, m * 2 + dz)
                    at = (half, *where, slice(t * 16, t * 16 + 16), cols)
                    even, uneven = g[row : row + 16], g[row + 16 : row + 32]
                    mine[at] = jnp.where(odd, uneven, even).astype(BF16)
                    other[at] = jnp.where(odd, even, uneven).astype(BF16)
        side = left if n < 2 else right
        g = dot_rows(gated[...], side[:, cols])
        order = Z_ORDERS[half] if layer == 1 else Z_ORDER
        for unit in range(4):
            for y in range(Y):
                where, _ = place(layer, half, y, order[2 * unit])
                at = (half, *where, slice(32, 48), cols)
                mine_parts, other_parts = [], []
                for t in range(2):
                    row = order[unit * 2 + t] * 64 + y * 16
                    even, uneven = g[row : row + 8], g[row + 8 : row + 16]
                    mine_parts.append(jnp.where(odd_8, uneven, even))
                    other_parts.append(jnp.where(odd_8, even, uneven))
                mine[at] = jnp.concatenate(mine_parts, axis=0).astype(BF16)
                other[at] = jnp.concatenate(other_parts, axis=0).astype(BF16)
        if n % 2 == 1:
            copies[half].start()
    for copy in copies:
        copy.wait()


def gradient_1_kernel(core, *refs):
    gradient_body(core, 1, *refs)


def gradient_0_kernel(
    core, halo, local, gated_low, gated_high, pre_low, pre_high, left_low, left_high, right,
    mine, sent,
    stream, gated, pre, left, other, sems,
):
    stream[:D0, :] = halo[D1:, :]
    stream[D0:, :] = local[...]
    gated[:D0, :] = gated_low[...]
    gated[D0:, :] = gated_high[...]
    pre[:TILE, :] = pre_low[...]
    pre[TILE:, :] = pre_high[...]
    left[:TILE, :] = left_low[...]
    left[TILE:, :] = left_high[...]
    gradient_body(core, 0, stream, gated, pre, left, right, mine, sent, other, sems)


def kernel_call(kernel, shapes, args, flops, moved, limit, scratch=(), smem=0, sent=0):
    vmem = pl.BlockSpec(memory_space=pltpu.VMEM)
    return pl.pallas_call(
        kernel,
        out_shape=[jax.ShapeDtypeStruct(s, t) for s, t in shapes],
        in_specs=[pl.BlockSpec(memory_space=pltpu.SMEM)] * smem + [vmem] * (len(args) - smem),
        out_specs=[vmem] * (len(shapes) - sent) + [pl.BlockSpec(memory_space=pl.ANY)] * sent,
        scratch_shapes=scratch,
        compiler_params=pltpu.CompilerParams(vmem_limit_bytes=limit * MIB),
        cost_estimate=pl.CostEstimate(flops=flops, bytes_accessed=moved, transcendentals=0),
    )(*args)


def halve(parts, axis, pairs, bit):
    kept = lax.dynamic_index_in_dim(parts, bit, 0, False, allow_negative_indices=False)
    sent = lax.dynamic_index_in_dim(parts, 1 - bit, 0, False, allow_negative_indices=False)
    got = lax.ppermute(sent, axis, list(enumerate(pairs)))
    return (kept.astype(F32) + got.astype(F32)).astype(BF16)


def picked(parts, i):
    return lax.dynamic_index_in_dim(parts, i, 0, False, allow_negative_indices=False)


def halve_of_two(terms, axis, pairs, bit):
    sent = sum(picked(t, 1 - bit).astype(F32) for t in terms).astype(BF16)
    got = lax.ppermute(sent, axis, list(enumerate(pairs)))
    return (sum(picked(t, bit).astype(F32) for t in terms) + got.astype(F32)).astype(BF16)


def split(s):
    return s.reshape((2, 2) + s.shape[1:])


def split_last(s):
    lead = s.shape[:-2]
    conv, out = s[..., :32, :].reshape(*lead, 2, 16, CH), s[..., 32:, :].reshape(*lead, 2, 8, CH)
    return jnp.moveaxis(jnp.concatenate([conv, out], axis=-2), -3, 0)


def together(a, b):
    return lax.optimization_barrier((a, b))


def from_x(s):
    return [lax.ppermute(s, "x", [(i, (i + k) % X) for i in range(X)]) for k in (2, 1, 3)]


def along(value, steps):
    initial, last = (max(0, -steps), min(X, X - steps))
    return lax.ppermute(value, "x", [(s, s + steps) for s in range(initial, last)])


def assemble_kernel(own, opposite, one, two, conv, out):
    for layer in range(2):
        for half in range(2):
            i = 2 * layer + half
            at = slice(half * CH, half * CH + CH)
            piece = (own[i].astype(F32) + opposite[i].astype(F32)) + (one[i].astype(F32) + two[i].astype(F32))
            conv[layer, :, at] = piece[:16]
            out[layer, :, at] = piece[16:]


def ring_bits(i):
    b = i >> 1
    return (i + b) & 1, b


def on_device(resid_in, conv_weight, out_weight, resid_cot, skip_cot):
    x0, rc, sc = resid_in[0], resid_cot[0], skip_cot[0]
    core = lax.axis_index("c")[None]
    yi, zi = lax.axis_index("y"), lax.axis_index("z")
    ya, yb = ring_bits(yi)
    z_bits = [(((i + 1) >> 1) & 1, (Z_SECOND >> i) & 1, (Z_THIRD >> i) & 1) for i in (zi, (zi - 1) & (Z - 1))]
    high = ROWS - D0
    halo = along(x0[ROWS - HALO :], 1)
    stream_high, gated_high, high_f, high_g, skip_high = kernel_call(
        forward_local_kernel,
        [((high, CH), BF16)] * 2 + [((high, CH), F32)] * 3,
        (x0, conv_weight, out_weight),
        12 * 10**8,
        10**7,
        16,
    )
    halo, high_f = lax.optimization_barrier((halo, high_f))
    early1, pre1_low, stream1, gated_low, gated1_low, low_f, low_g = kernel_call(
        forward_low_kernel,
        [((D1, CH), BF16), ((TILE, 2 * CH), BF16), ((ROWS + D1, CH), BF16)]
        + [((D0, CH), BF16), ((TILE, CH), BF16)]
        + [((D0, CH), F32)] * 2,
        (halo, x0, conv_weight, out_weight, rc, sc, stream_high),
        2 * 10**9,
        10**7,
        16,
        [pltpu.VMEM((HALO + D0, CH), BF16)],
    )
    returned1 = along(early1, -1)
    flow1_low, flow1_high, pre1, gated1, skip = kernel_call(
        forward_high_kernel,
        [((TILE, CH), F32)] * 2 + [((ROWS, 2 * CH), BF16), ((ROWS, CH), BF16), ((ROWS, CH), BF16)],
        (stream1, conv_weight, out_weight, rc, sc, skip_high, gated_low, gated1_low, pre1_low),
        5 * 10**9,
        10**7,
        16,
    )
    pieces = (4, 4, 48, CH)
    own_copy = [pltpu.VMEM((2,) + pieces, BF16), pltpu.SemaphoreType.DMA((2,))]
    mine1, other1 = kernel_call(
        gradient_1_kernel,
        [((2,) + pieces, BF16)] * 2,
        (core, stream1, gated1, pre1, rc, sc),
        5 * 10**9,
        6 * 10**6,
        16,
        own_copy,
        smem=1,
        sent=1,
    )
    proj_low, pre_low, flow_low, early0 = kernel_call(
        backward_low_kernel,
        [((TILE, CH), BF16), ((TILE, 2 * CH), BF16), ((TILE, CH), F32), ((D0, CH), BF16)],
        (flow1_low, low_f, low_g, high_f, high_g, sc, out_weight, conv_weight),
        25 * 10**8,
        6 * 10**6,
        16,
    )
    returned1, mine1, flow_low = lax.optimization_barrier((returned1, mine1, flow_low))
    proj_high, pre_high, resid_most, tail = kernel_call(
        backward_high_kernel,
        [((TILE, CH), BF16), ((TILE, 2 * CH), BF16), ((high, CH), BF16), ((D0, CH), F32)],
        (flow1_high, returned1, high_f, high_g, sc, out_weight, conv_weight, flow_low),
        25 * 10**8,
        6 * 10**6,
        16,
    )
    got1 = lax.ppermute(other1, "c", [(0, 1), (1, 0)])
    mine0, other0 = kernel_call(
        gradient_0_kernel,
        [((2,) + pieces, BF16)] * 2,
        (core, halo, x0, gated_low, gated_high, pre_low, pre_high, proj_low, proj_high, sc),
        5 * 10**9,
        6 * 10**6,
        16,
        [pltpu.VMEM((ROWS + D0, CH), BF16), pltpu.VMEM((ROWS, CH), BF16)]
        + [pltpu.VMEM((ROWS, 2 * CH), BF16), pltpu.VMEM((ROWS, CH), BF16)]
        + own_copy,
        smem=1,
        sent=1,
    )
    got0 = lax.ppermute(other0, "c", [(0, 1), (1, 0)])

    pairs_1 = (Z_PAIRS, Z_PAIRS_NEXT)
    y_steps = ((FIRST, ya), (SECOND, yb))
    s1 = [
        halve_of_two((split(mine1[half]), split(got1[half])), "z", pairs_1[half][0], z_bits[half][0])
        for half in range(2)
    ]
    s0 = [halve_of_two((split(mine0[half]), split(got0[half])), "y", *y_steps[half]) for half in range(2)]
    s0, s1 = together(s0, s1)
    early0, s0 = together(early0, s0)
    returned0 = along(early0, -1)
    resid = jnp.concatenate([resid_most, (tail + returned0.astype(F32)).astype(BF16)])
    s0 = [halve(s0[half], "y", *y_steps[1 - half]) for half in range(2)]
    s1 = [halve(s1[half], "z", pairs_1[half][1], z_bits[half][1]) for half in range(2)]
    s0, s1 = together(s0, s1)
    s0 = halve(split(jnp.stack(s0, axis=1)), "z", Z_PAIRS[0], z_bits[0][0])
    s1 = halve(split(jnp.stack(s1, axis=1)), "y", *y_steps[0])
    s0, s1 = together(s0, s1)
    s0 = halve(s0, "z", Z_PAIRS[1], z_bits[0][1])
    s1 = halve(s1, "y", *y_steps[1])
    most, least = together(jnp.concatenate([s0, s1[:1]]), s1[1:])
    most = halve(split_last(most), "z", Z_PAIRS[2], z_bits[0][2])
    least = halve(split_last(least), "z", Z_PAIRS_NEXT[2], z_bits[1][2])
    s = jnp.concatenate([most, least])
    conv_grad, out_grad = kernel_call(
        assemble_kernel,
        [((2, 16, 1024), F32), ((2, 8, 1024), F32)],
        [s] + from_x(s),
        10**6,
        10**6,
        8,
    )
    return conv_grad, out_grad, resid[None], skip[None]


def solution(mesh):
    fine = Mesh(mesh.devices.reshape(Z, Y, CORES, X), ("z", "y", "c", "x"))
    dp = ("z", "y", "c")
    return jax.shard_map(
        on_device,
        mesh=fine,
        in_specs=(P(dp, "x", None), P(), P(), P(dp, "x", None), P(dp, "x", None)),
        out_specs=(P(None, dp, None), P(None, dp, None), P(dp, "x", None), P(dp, "x", None)),
        check_vma=False,
    )
```
